32 devices in a mesh: dp: 16 (over z, y, x), tensor: 2 (over core).
Axes of the slice: x: 2, y: 2, z: 4, core: 2. Of those that a mesh axis runs over, the one named last changes fastest.
Arguments:
- tokens: bfloat16 [16384, 512], P(('dp', 'tensor')), may hold values from -6 to 6
- first_cotangent: bfloat16 [16384, 512], P(('dp', 'tensor')), may hold values from -6 to 6
- second_cotangent: bfloat16 [16384, 512], P(('dp', 'tensor')), may hold values from -6 to 6
- projection: bfloat16 [3, 512, 512], P(None, None, 'tensor'), may hold values from -0.25 to 0.25
- offsets: float32 [2, 512], P(None, 'tensor'), may hold values from -3 to 3
- combiner: bfloat16 [512, 512], P('tensor'), may hold values from -2 to 2
- baseline: float32 [512], replicated, may hold values from -3 to 3
- scales: float32 [512], replicated, may hold values from 0.25 to 1.75
- shifts: float32 [512], replicated, may hold values from -3 to 3
- expander: bfloat16 [512, 512], P(None, 'tensor'), may hold values from -0.25 to 0.25
- thresholds: bfloat16 [512], P('tensor'), may hold values from -3 to 3
- reducer: bfloat16 [512, 512], P('tensor'), may hold values from -0.25 to 0.25
- adjustment: float32 [512], replicated, may hold values from -3 to 3
- rescales: float32 [512], replicated, may hold values from 0.25 to 1.75
- reshifts: float32 [512], replicated, may hold values from -3 to 3
- known_flags: int32 [16384], P('dp'), may hold values 0 or 1
- chosen_flags: int32 [16384], P('dp'), may hold values 0 or 1
- cell_lengths: int32 [16, 4], P('dp'), may hold values from 1 to 682, 1024 in all within a row
Outputs:
- first_pass: bfloat16 [16384, 512], P(('dp', 'tensor'))
- second_pass: bfloat16 [16384, 512], P(('dp', 'tensor'))
- tokens_gradient: float32 [16384, 512], P(('dp', 'tensor'))
- projection_gradient: float32 [3, 512, 512], P(None, None, 'tensor')
- offsets_gradient: float32 [2, 512], P(None, 'tensor')
- combiner_gradient: float32 [512, 512], P('tensor')
- baseline_gradient: float32 [512], replicated
- scales_gradient: float32 [512], replicated
- shifts_gradient: float32 [512], replicated
- expander_gradient: float32 [512, 512], P(None, 'tensor')
- thresholds_gradient: float32 [512], P('tensor')
- reducer_gradient: float32 [512, 512], P('tensor')
- adjustment_gradient: float32 [512], replicated
- rescales_gradient: float32 [512], replicated
- reshifts_gradient: float32 [512], replicated
The draws below stay inside these ranges and needn't reach their ends.
Inputs may be any that keep to these rules, and one draw needn't show every extreme that they name: `cell_lengths`: row g holds the lengths of the 4 cells of data group g in order; each row sums to 1024 and its largest entry is exactly 682.
All inputs are finite; a program needn't handle non-finite values. No bound on the sum of `known_flags` or of `chosen_flags` on one device may be relied on, other than what follows from the above.
Results may differ from the reference program's by a relative error of at most 0.019.
Values may be sent and summed in bfloat16 or wider, within the bound.
No kernel may reach another device: no remote copies, remote signals or barrier semaphores. Data moves between devices by JAX's collectives and lax.ppermute only.
A program may use at most 128 MiB of HBM per device.

```python
import math
import jax
import jax.numpy as jnp
import numpy as np
from jax import lax

D = 512
HEADS = 8
FF = 512
HD = 64
TOK_DEV = 1024
CELLS_DEV = 4
CELL_MOST = 682
TOKENS = 16384
N_DP = 16


def with_ends(entries, own_key, least, largest):
    index_at = [jax.random.randint(jax.random.fold_in(own_key, axis), (), 0, length) for axis, length in enumerate(entries.shape)]
    widest = entries.shape.index(max(entries.shape))
    neighbour = index_at[:widest] + [(index_at[widest] + 1) % entries.shape[widest]] + index_at[widest + 1:]
    return entries.at[tuple(index_at)].set(least).at[tuple(neighbour)].set(largest)


def shard_levels(rng, shape, shards, low, high):
    factor_of = 1.0
    for position, shards_of in shards:
        heights = jax.random.uniform(jax.random.fold_in(jax.random.fold_in(rng, 6), position), (shards_of,), jnp.float32, low / len(shards), high / len(shards))
        factor_of = factor_of * jnp.repeat(jnp.exp(heights), shape[position] // shards_of).reshape((-1,) + (1,) * (len(shape) - 1 - position))
    return factor_of


def profile(count, total, most, skew):
    portions = [(1 << 20) // math.isqrt(grade ** skew) + 1 for grade in range(2, count + 1)]
    rest, counts = total - most - (count - 1), [1] * (count - 1)
    while rest > 0:
        candidates = [i for i in range(count - 1) if counts[i] < most]
        pool, budget = sum([portions[i] for i in candidates]), rest
        for i in candidates:
            more = min(most - counts[i], max(1, budget * portions[i] // pool), rest)
            counts[i] = counts[i] + more
            rest = rest - more
    return np.array([most] + counts)


def ragged(rng, count, total, bound, slope):
    if count == 2:
        one = jax.random.randint(rng, (), max(1, total - bound), min(bound, total - 1) + 1)
        return jnp.stack([one, total - one])
    lengths = jnp.asarray(profile(count, total, bound, slope), jnp.int32)
    pairs = (count - 1) // 2
    source_of, sink = lengths[1:1 + 2 * pairs:2], lengths[2:2 + 2 * pairs:2]
    margin = jnp.minimum(source_of - 1, bound - sink)
    shifted = jax.random.randint(jax.random.fold_in(rng, 1), (pairs,), 0, 1 << 20) % (margin + 1)
    lengths = lengths.at[1:1 + 2 * pairs:2].set(source_of - shifted).at[2:2 + 2 * pairs:2].set(sink + shifted)
    return lengths[jax.random.permutation(jax.random.fold_in(rng, 2), count)]


def scatter_about(key, extent, deviation, bound, split=(), kind=jnp.bfloat16):
    factor_of = shard_levels(key, extent, split, -0.22, 0.18) if split else 1.0
    drawn = jax.random.normal(key, extent, jnp.float32) * deviation * factor_of
    return jnp.minimum(jnp.maximum(drawn, -bound), bound).astype(kind)


def setup_inputs(seed: int = 0) -> dict:
    splits = jax.random.split(jax.random.key(seed), 19)
    tokens = scatter_about(splits[0], (TOKENS, D), 1.0, 6.0, ((0, 32),))
    first_cotangent = scatter_about(splits[1], (TOKENS, D), 1.0, 6.0, ((0, 32),))
    second_cotangent = scatter_about(splits[2], (TOKENS, D), 1.0, 6.0, ((0, 32),))
    projection = scatter_about(splits[3], (3, D, D), D ** -0.5, 0.25, ((2, 2),))
    offsets = scatter_about(splits[4], (2, D), 0.3, 3.0, ((1, 2),), jnp.float32)
    combiner = scatter_about(splits[5], (D, D), 8 ** -0.5, 2.0, ((0, 2),))
    baseline = scatter_about(splits[6], (D,), 0.3, 3.0, (), jnp.float32)
    scales = jnp.clip(1.0 + 0.15 * jax.random.normal(splits[7], (D,), jnp.float32), 0.25, 1.75)
    shifts = scatter_about(splits[8], (D,), 0.3, 3.0, (), jnp.float32)
    expander = scatter_about(splits[9], (D, FF), D ** -0.5, 0.25, ((1, 2),))
    thresholds = scatter_about(splits[10], (FF,), 0.3, 3.0, ((0, 2),))
    reducer = scatter_about(splits[11], (FF, D), FF ** -0.5, 0.25, ((0, 2),))
    adjustment = scatter_about(splits[12], (D,), 0.3, 3.0, (), jnp.float32)
    rescales = jnp.clip(1.0 + 0.15 * jax.random.normal(splits[13], (D,), jnp.float32), 0.25, 1.75)
    reshifts = scatter_about(splits[14], (D,), 0.3, 3.0, (), jnp.float32)
    known_flags = with_ends((jax.random.randint(splits[15], (TOKENS,), 0, 2) < 1).astype(jnp.int32), jax.random.fold_in(splits[15], 1), 0, 1)
    chosen_flags = with_ends((jax.random.randint(splits[16], (TOKENS,), 0, 4) < 1).astype(jnp.int32), jax.random.fold_in(splits[16], 1), 0, 1)
    cell_lengths = jax.vmap(lambda own: ragged(own, CELLS_DEV, TOK_DEV, CELL_MOST, 2))(jax.random.split(splits[17], N_DP)).reshape((N_DP, CELLS_DEV)).astype(jnp.int32)
    return {"tokens": tokens, "first_cotangent": first_cotangent, "second_cotangent": second_cotangent, "projection": projection, "offsets": offsets, "combiner": combiner, "baseline": baseline, "scales": scales, "shifts": shifts, "expander": expander, "thresholds": thresholds, "reducer": reducer, "adjustment": adjustment, "rescales": rescales, "reshifts": reshifts, "known_flags": known_flags, "chosen_flags": chosen_flags, "cell_lengths": cell_lengths}


@jax.custom_vjp
def low(v):
    return lax.optimization_barrier(v.astype(jnp.bfloat16)).astype(jnp.float32)

@jax.custom_vjp
def low_back(v):
    return v

def low_keep(v):
    return (low(v), None)

def low_pass(kept, grad):
    return (grad,)

def back_keep(v):
    return (v, None)

def back_low(kept, grad):
    return (low(grad),)
low.defvjp(low_keep, low_pass)
low_back.defvjp(back_keep, back_low)

def matmul(left, right):
    return jnp.dot(left, right, precision=lax.Precision.HIGHEST)

def layer_norm(values, norm_gain, norm_shift):
    centered = values - lax.optimization_barrier(jnp.mean(values, axis=-1, keepdims=True))
    spread_sq = lax.optimization_barrier(jnp.mean(centered * centered, axis=-1, keepdims=True))
    return centered * lax.rsqrt(spread_sq + 1e-05) * norm_gain + norm_shift

def attention(queries, keys_all, values_all, segment, visible):
    total_rows = queries.shape[0]
    block_rows = min(512, total_rows)
    positions = jnp.arange(total_rows, dtype=jnp.int32)
    shaped_queries = queries.reshape(total_rows, HEADS, HD)
    shaped_keys = keys_all.reshape(total_rows, HEADS, HD)
    shaped_values = values_all.reshape(total_rows, HEADS, HD)

    def one_block(block_index):
        row_start = block_index * block_rows
        query_block = lax.dynamic_slice_in_dim(shaped_queries, row_start, block_rows, 0)
        own_cells = lax.dynamic_slice_in_dim(segment, row_start, block_rows, 0)
        own_rows = row_start + jnp.arange(block_rows, dtype=jnp.int32)
        allowed = (own_cells[:, None] == segment[None, :]) & (visible[None, :] | (own_rows[:, None] == positions[None, :]))
        scores = low_back(jnp.einsum('qhd,khd->hqk', query_block, shaped_keys, precision=lax.Precision.HIGHEST) * HD ** (-0.5))
        scores = jnp.where(allowed[None], scores, -1e+30)
        weights = jnp.exp(scores - lax.optimization_barrier(jnp.max(scores, axis=-1, keepdims=True)))
        probability = weights / lax.optimization_barrier(jnp.sum(weights, axis=-1, keepdims=True))
        return jnp.einsum('hqk,khd->qhd', low(probability), shaped_values, precision=lax.Precision.HIGHEST)
    blocks = lax.map(jax.checkpoint(one_block), jnp.arange(total_rows // block_rows, dtype=jnp.int32))
    return blocks.reshape(total_rows, HEADS * HD)

def layer(entry_rows, visible, segment, params):
    projection, offsets, combiner, baseline, scales, shifts, expander, thresholds, reducer, adjustment, rescales, reshifts = params
    entry_low = low(entry_rows)
    queries = low(low_back(matmul(entry_low, projection[0]) + offsets[0]))
    keys_all = low(low_back(matmul(entry_low, projection[1])))
    values_all = low(low_back(matmul(entry_low, projection[2]) + offsets[1]))
    context = low(low_back(attention(queries, keys_all, values_all, segment, visible)))
    mixture = entry_rows + low_back(matmul(context, combiner)) + baseline
    normed = layer_norm(mixture, scales, shifts)
    before = low_back(matmul(low(normed), expander) + thresholds)
    hidden = low(jax.nn.gelu(before, approximate=False))
    summed = normed + low_back(matmul(hidden, reducer)) + adjustment
    return layer_norm(summed, rescales, reshifts)

def reference(tokens, first_cotangent, second_cotangent, projection, offsets, combiner, baseline, scales, shifts, expander, thresholds, reducer, adjustment, rescales, reshifts, known_flags, chosen_flags, cell_lengths):
    params = tuple((member.astype(jnp.float32) for member in (projection, offsets, combiner, baseline, scales, shifts, expander, thresholds, reducer, adjustment, rescales, reshifts)))

    def one_group(totals, group_index):
        row_start = group_index * TOK_DEV

        def select_rows(source):
            return lax.dynamic_slice_in_dim(source, row_start, TOK_DEV, 0)
        entry_rows = select_rows(tokens).astype(jnp.float32)
        visible = select_rows(known_flags) > 0
        chosen = select_rows(chosen_flags) > 0
        cell_ends = jnp.cumsum(lax.dynamic_index_in_dim(cell_lengths, group_index, 0, keepdims=False)).astype(jnp.int32)
        positions = jnp.arange(TOK_DEV, dtype=jnp.int32)
        segment = lax.optimization_barrier(jnp.sum((positions[:, None] >= cell_ends[None, :]).astype(jnp.int32), axis=1)).astype(jnp.int32)

        def forward(entry_values, weight_values):
            first_out = low(layer(entry_values, visible, segment, weight_values))
            second_entry = jnp.where(chosen[:, None], first_out, entry_values)
            second_out = layer(second_entry, visible | chosen, segment, weight_values)
            return (first_out, second_out)
        outputs, pullback = jax.vjp(forward, entry_rows, params)
        entry_slope, weight_slopes = pullback((select_rows(first_cotangent).astype(jnp.float32), select_rows(second_cotangent).astype(jnp.float32)))
        totals = jax.tree.map(jnp.add, totals, weight_slopes)
        return (totals, (outputs[0].astype(jnp.bfloat16), outputs[1].astype(jnp.bfloat16), entry_slope))
    start_totals = jax.tree.map(jnp.zeros_like, params)
    totals, (first_out, second_out, entry_slopes) = lax.scan(one_group, start_totals, jnp.arange(N_DP, dtype=jnp.int32))
    return (first_out.reshape(TOKENS, D), second_out.reshape(TOKENS, D), entry_slopes.reshape(TOKENS, D), totals[0], totals[1], totals[2], totals[3], totals[4], totals[5], totals[6], totals[7], totals[8], totals[9], totals[10], totals[11])
```

```python
import functools
import types

import jax
import jax.numpy as jnp
from jax import lax
from jax.experimental import pallas as pl
from jax.experimental.pallas import tpu as pltpu
from jax.sharding import PartitionSpec as P

HD = 64
PAIR = 2 * HD
BF = jnp.bfloat16
F32 = jnp.float32
HIDE = -1e30
SAFE = 60.0
LEAST = 1e-26
NN = (((1,), (0,)), ((), ()))
NT = (((1,), (1,)), ((), ()))
TN = (((0,), (0,)), ((), ()))
LIMITS = {"first_kernel": 58, "second_kernel": 58, "back_kernel": 58, "small": 24}
UNROLL_FORWARD = 2
UNROLL_BACKWARD = 1
Q_TILE = 256
K_TILE = 256
WINDOWS = (128, 256, 384, 512, 640)


def dot(left, right, dims=NN):
    return lax.dot_general(left, right, dims, preferred_element_type=F32)


def lanes_of(rows):
    return lax.broadcasted_iota(jnp.int32, (rows, PAIR), 1)


def cells_of(meta):
    return (meta.shape[0] - 1) // 3


def row_cells(start, rows, meta, bounds):
    position = start + lax.broadcasted_iota(jnp.int32, (rows, PAIR), 0)
    cell = jnp.zeros((rows, PAIR), jnp.int32)
    for c in bounds:
        cell = cell + (position >= meta[c]).astype(jnp.int32)
    return cell


def norm_forward(values, gain, shift):
    centered = values - jnp.mean(values, axis=-1, keepdims=True)
    inverse = lax.rsqrt(jnp.mean(centered * centered, axis=-1, keepdims=True) + 1e-05)
    unit = centered * inverse
    return unit * gain + shift, unit, inverse


def norm_backward(gradient, unit, inverse, gain):
    scaled = gradient * gain
    projected = (
        scaled
        - jnp.mean(scaled, axis=-1, keepdims=True)
        - unit * jnp.mean(scaled * unit, axis=-1, keepdims=True)
    )
    return (
        projected * inverse,
        jnp.sum(gradient * unit, axis=0, keepdims=True),
        jnp.sum(gradient, axis=0, keepdims=True),
    )


def key_marks(meta, turn, marks_ref):
    rows = marks_ref.shape[0]
    n_cells = cells_of(meta)
    lane = lanes_of(rows)
    first = 1 + n_cells * (1 + turn)
    cell = row_cells(0, rows, meta, range(first, first + n_cells))
    marks_ref[...] = jnp.where(
        lane < n_cells,
        jnp.where(cell == lane, 0.0, HIDE),
        jnp.where((lane % HD >= n_cells) & (lane % HD < n_cells + 3), -1.0, 0.0),
    ).astype(BF)


def flag_column(meta, flags, row, rows):
    pick = (lax.broadcasted_iota(jnp.int32, (flags.shape[0], PAIR), 0) == row).astype(BF)
    start = pl.multiple_of(meta[0] * rows, rows)
    return dot(flags[:, pl.ds(start, rows)], pick, TN)


def key_tiles(meta, turn):
    count = meta[n_bounds(meta, turn)]
    return jnp.maximum((count + K_TILE - 1) // K_TILE, 1)


def n_bounds(meta, turn):
    return cells_of(meta) * (2 + turn)


def select_keys(meta, turn, ranks, sel_ref):
    keys_all = ranks.shape[1]
    tiles = key_tiles(meta, turn)
    place = ranks[turn : turn + 1, :]
    for tile in range(keys_all // K_TILE):

        @pl.when(tile < tiles)
        def _():
            row = (lax.broadcasted_iota(jnp.int32, (K_TILE, keys_all), 0) + tile * K_TILE).astype(F32)
            sel_ref[tile * K_TILE : (tile + 1) * K_TILE, :] = (row == place).astype(BF)


def spread_pairs(ref, side, half, at, values):
    for part in range(half // PAIR):
        ref[side * (half // PAIR) + part, at, :] = values[:, part * PAIR : (part + 1) * PAIR]


def project(meta, turn, entry_own, entry_all, weights_ref, vec, sel_ref, q_ref, k_ref, v_ref, ko_ref, vo_ref):
    half = weights_ref.shape[3]
    every = slice(None)
    for side in range(2):
        cols = slice(side * half, (side + 1) * half)
        queries = (dot(entry_own, weights_ref[side, 0]) + vec[7:8, cols]).astype(BF) * 0.125
        spread_pairs(q_ref, side, half, every, queries.astype(BF))
        spread_pairs(ko_ref, side, half, every, dot(entry_own, weights_ref[side, 1]).astype(BF))
        spread_pairs(vo_ref, side, half, every, (dot(entry_own, weights_ref[side, 2]) + vec[8:9, cols]).astype(BF))
    tiles = key_tiles(meta, turn)
    for tile in range(entry_all.shape[0] // K_TILE):
        at = slice(tile * K_TILE, (tile + 1) * K_TILE)

        @pl.when(tile < tiles)
        def _():
            entry = dot(sel_ref[at, :], entry_all[...]).astype(BF)
            for side in range(2):
                cols = slice(side * half, (side + 1) * half)
                spread_pairs(k_ref, side, half, at, dot(entry, weights_ref[side, 1]).astype(BF))
                spread_pairs(v_ref, side, half, at, (dot(entry, weights_ref[side, 2]) + vec[8:9, cols]).astype(BF))

        @pl.when(tile >= tiles)
        def _():
            k_ref[:, at, :] = jnp.zeros((k_ref.shape[0], K_TILE, PAIR), BF)
            v_ref[:, at, :] = jnp.zeros((v_ref.shape[0], K_TILE, PAIR), BF)


def for_windows(meta, turn, rows, keys_all, body):
    n_cells = cells_of(meta)
    ends, seen = 1, 1 + n_cells * (1 + turn)

    def one_tile(tile, carried):
        first = meta[0] * rows + tile * Q_TILE
        last = first + Q_TILE - 1
        low, high = 0, meta[seen + n_cells - 1]
        for c in range(n_cells - 1):
            low = jnp.where(first >= meta[ends + c], meta[seen + c], low)
            d = n_cells - 2 - c
            high = jnp.where(last < meta[ends + d], meta[seen + d], high)
        low = (low // 16) * 16
        need = high - low
        below = -1
        for width in WINDOWS + (keys_all,):
            start = pl.multiple_of(jnp.minimum(low, keys_all - width), 16)

            @pl.when((need > below) & (need <= width))
            def _():
                body(tile, start, width)

            below = width
        return carried

    lax.fori_loop(0, rows // Q_TILE, one_tile, 0)


def head_sums(values):
    high = values.astype(BF)
    low = (values - high.astype(F32)).astype(BF)
    row = lax.broadcasted_iota(jnp.int32, (2 * PAIR, PAIR), 0) % PAIR
    lane = lax.broadcasted_iota(jnp.int32, (2 * PAIR, PAIR), 1)
    ones = ((row < HD) == (lane < HD)).astype(BF)
    return dot(jnp.concatenate([high, low], axis=1), ones)


def by_head(values):
    lane = lax.broadcasted_iota(jnp.int32, values.shape, 1)
    zero = jnp.zeros_like(values)
    return jnp.concatenate([jnp.where(lane < HD, values, zero), jnp.where(lane < HD, zero, values)], axis=0)


def merge_heads(values):
    rows = values.shape[0] // 2
    lane = lanes_of(rows)
    return jnp.where(lane < HD, values[:rows], values[rows:])


def own_places(meta, first, rows):
    n_cells = cells_of(meta)
    lane = lanes_of(rows)
    cell = row_cells(first, rows, meta, range(1, n_cells))
    return jnp.where((cell == lane) & (lane < n_cells), 1.0, 0.0)


def row_tails(place, offset, n_cells):
    lane = lanes_of(offset.shape[0])
    side = lane % HD
    high = offset.astype(BF).astype(F32)
    middle = (offset - high).astype(BF).astype(F32)
    taken = jnp.where(
        side == n_cells,
        high,
        jnp.where(side == n_cells + 1, middle, jnp.where(side == n_cells + 2, offset - high - middle, 0.0)),
    )
    return jnp.concatenate(
        [jnp.where(lane < HD, taken, 0.0) + place, jnp.where(lane < HD, 0.0, taken) + place], axis=0
    ).astype(BF)


def attend(meta, turn, flags, q_ref, k_ref, v_ref, ko_ref, vo_ref, marks_ref, closed_ref, off_ref, top_ref, edge_ref, ctx_ref, lse_ref):
    pairs, rows = q_ref.shape[0], q_ref.shape[1]
    n_cells = cells_of(meta)
    lane = lanes_of(Q_TILE)
    closed_ref[...] = jnp.where(flag_column(meta, flags, turn, rows) > 0.5, HIDE, 0.0)
    off_ref[...] = jnp.zeros_like(off_ref)

    def own_scores(pair, at):
        product = q_ref[pair, at, :].astype(F32) * ko_ref[pair, at, :].astype(F32)
        return head_sums(product) + closed_ref[at, :] - off_ref[pair, at, :]

    def one_tile(tile, start, width):
        at = pl.ds(pl.multiple_of(tile * Q_TILE, Q_TILE), Q_TILE)
        place = own_places(meta, meta[0] * rows + tile * Q_TILE, Q_TILE)
        window = pl.ds(start, width)

        def one_pair(pair, carried):
            offset = off_ref[pair, at, :]
            keys = jnp.concatenate([k_ref[pair, window, :], marks_ref[window, :]], axis=1)
            vals = jnp.concatenate([v_ref[pair, window, :], jnp.ones((width, PAIR), BF)], axis=1)
            asked = jnp.concatenate([by_head(q_ref[pair, at, :]), row_tails(place, offset, n_cells)], axis=1)
            scores = dot(asked, keys, NT)
            mixed = dot(jnp.exp(scores).astype(BF), vals)
            top = scores[:, :PAIR]
            for part in range(1, width // PAIR):
                top = jnp.maximum(top, scores[:, part * PAIR : (part + 1) * PAIR])
            top_ref[pair, tile] = top
            self_score = own_scores(pair, at)
            self_weight = jnp.exp(self_score)
            total = merge_heads(mixed[:, PAIR:]) + self_weight
            context = (merge_heads(mixed[:, :PAIR]) + self_weight * vo_ref[pair, at, :].astype(F32)) / total
            ctx_ref[pair, at, :] = context.astype(BF)
            lse_ref[pair, at, :] = offset + jnp.log(total)
            highest = jnp.maximum(jnp.maximum(top[:Q_TILE], top[Q_TILE:]), self_score)
            edge_ref[0] = jnp.maximum(edge_ref[0], jnp.max(highest.reshape(-1, 8, PAIR), axis=0))
            edge_ref[1] = jnp.minimum(edge_ref[1], jnp.min(total.reshape(-1, 8, PAIR), axis=0))
            return carried

        lax.fori_loop(0, pairs, one_pair, 0, unroll=UNROLL_FORWARD)

    def attempt(_):
        edge_ref[0] = jnp.full(edge_ref.shape[1:], HIDE, F32)
        edge_ref[1] = jnp.ones(edge_ref.shape[1:], F32)
        for_windows(meta, turn, rows, k_ref.shape[1], one_tile)
        again = (jnp.max(edge_ref[0]) > SAFE) | (jnp.min(edge_ref[1]) < LEAST)

        @pl.when(again)
        def _():
            def raise_pair(index, carried):
                tile, pair = index // pairs, index % pairs
                at = pl.ds(pl.multiple_of(tile * Q_TILE, Q_TILE), Q_TILE)
                top = jnp.max(top_ref[pair, tile], axis=1, keepdims=True)
                tops = jnp.where(lane < HD, top[:Q_TILE], top[Q_TILE:])
                off_ref[pair, at, :] = off_ref[pair, at, :] + jnp.maximum(tops, own_scores(pair, at))
                return carried

            lax.fori_loop(0, pairs * (rows // Q_TILE), raise_pair, 0)

        return again.astype(jnp.int32)

    lax.while_loop(lambda again: again > 0, attempt, jnp.int32(1))


def joined(ref):
    return jnp.concatenate([ref[i] for i in range(ref.shape[0])], axis=1)


def feed_forward(entry_own, ctx_ref, comb, exp_w, red, vec, before_ref, unit1_ref, unit2_ref, rs_ref):
    context = joined(ctx_ref)
    half = comb.shape[1]
    attended = dot(context[:, :half], comb[0]) + dot(context[:, half:], comb[1])
    mixture = entry_own.astype(F32) + attended + vec[0:1, :]
    normed, unit1, inverse1 = norm_forward(mixture, vec[1:2, :], vec[2:3, :])
    unit1_ref[...] = unit1
    normed_low = normed.astype(BF)
    summed = normed + vec[3:4, :]
    for side in range(2):
        cols = slice(side * half, (side + 1) * half)
        before = dot(normed_low, exp_w[side]) + vec[6:7, cols]
        before_ref[:, cols] = before
        hidden = (0.5 * before * (1.0 + lax.erf(before * 0.7071067811865476))).astype(BF)
        summed = summed + dot(hidden, red[side])
    result, unit2, inverse2 = norm_forward(summed, vec[4:5, :], vec[5:6, :])
    unit2_ref[...] = unit2
    rows = result.shape[0]
    rs_ref[...] = jnp.where(lanes_of(rows) < HD, inverse1, inverse2)
    return result


def feed_backward(incoming, before_ref, unit1_ref, unit2_ref, rs_ref, comb, exp_w, red, vec, hid_ref, sl_ref, nl_ref, bl_ref, ml_ref, do_ref):
    half = comb.shape[1]
    inverse1 = rs_ref[:, :1]
    inverse2 = rs_ref[:, PAIR - 1 :]
    summed_slope, rescale_part, reshift_part = norm_backward(
        incoming, unit2_ref[...], inverse2, vec[4:5, :]
    )
    summed_low = summed_slope.astype(BF)
    sl_ref[...] = summed_low
    unit1 = unit1_ref[...]
    nl_ref[...] = (unit1 * vec[1:2, :] + vec[2:3, :]).astype(BF)
    normed_slope = summed_slope
    threshold_parts = []
    for side in range(2):
        cols = slice(side * half, (side + 1) * half)
        before = before_ref[:, cols]
        phi = 0.5 * (1.0 + lax.erf(before * 0.7071067811865476))
        hid_ref[:, cols] = (before * phi).astype(BF)
        slope = phi + before * jnp.exp(-0.5 * before * before) * 0.3989422804014327
        before_low = (dot(summed_low, red[side], NT) * slope).astype(BF)
        bl_ref[:, cols] = before_low
        threshold_parts.append(jnp.sum(before_low.astype(F32), axis=0, keepdims=True))
        normed_slope = normed_slope + dot(before_low, exp_w[side], NT)
    mixture_slope, scales_part, shifts_part = norm_backward(
        normed_slope, unit1, inverse1, vec[1:2, :]
    )
    mixture_low = mixture_slope.astype(BF)
    ml_ref[...] = mixture_low
    for side in range(2):
        back = dot(mixture_low, comb[side], NT).astype(BF)
        for part in range(half // PAIR):
            do_ref[side * (half // PAIR) + part] = back[:, part * PAIR : (part + 1) * PAIR]
    sums = [
        jnp.sum(mixture_slope, axis=0, keepdims=True),
        scales_part,
        shifts_part,
        jnp.sum(summed_slope, axis=0, keepdims=True),
        rescale_part,
        reshift_part,
        jnp.concatenate(threshold_parts, axis=1),
    ]
    return mixture_slope, sums


def attend_backward(meta, turn, flags, q_ref, k_ref, v_ref, ko_ref, vo_ref, marks_ref, closed_ref, ctx_ref, lse_ref, do_ref, sel_ref,
                    dq_ref, dk_ref, dv_ref, dko_ref, dvo_ref, dkl_ref, dvl_ref):
    rows = q_ref.shape[1]
    n_cells = cells_of(meta)
    keys_all = k_ref.shape[1]
    lane = lanes_of(Q_TILE)
    closed_ref[...] = jnp.where(flag_column(meta, flags, turn, rows) > 0.5, HIDE, 0.0)
    dk_ref[...] = jnp.zeros_like(dk_ref)
    dv_ref[...] = jnp.zeros_like(dv_ref)

    def one_tile(tile, start, width):
        at = pl.ds(pl.multiple_of(tile * Q_TILE, Q_TILE), Q_TILE)
        place = own_places(meta, meta[0] * rows + tile * Q_TILE, Q_TILE)
        side = lane % HD
        window = pl.ds(start, width)
        def one_pair(pair, carried):
            q, back = q_ref[pair, at, :], do_ref[pair, at, :]
            qf, backf = q.astype(F32), back.astype(F32)
            k_own, v_own = ko_ref[pair, at, :].astype(F32), vo_ref[pair, at, :].astype(F32)
            k_pair = k_ref[pair, window, :]
            keys = jnp.concatenate([k_pair, marks_ref[window, :]], axis=1)
            vals = jnp.concatenate([v_ref[pair, window, :], jnp.ones((width, PAIR), BF)], axis=1)
            lse = lse_ref[pair, at, :]
            tails = row_tails(place, lse, n_cells)
            delta = head_sums(backf * ctx_ref[pair, at, :].astype(F32))
            high = delta.astype(BF).astype(F32)
            marks = jnp.where(side == 0, -high, jnp.where(side == 1, high - delta, 0.0)).astype(BF)
            q_two, back_two = by_head(q), by_head(back)
            probs = jnp.exp(dot(keys, jnp.concatenate([q_two, tails], axis=1), NT))
            slopes = dot(vals, jnp.concatenate([back_two, by_head(marks)], axis=1), NT)
            score_slope = (probs * slopes).astype(BF)
            dv_ref[pair, window, :] += dot(probs.astype(BF), back_two)
            dk_ref[pair, window, :] += dot(score_slope, q_two)
            dq = merge_heads(dot(score_slope, k_pair, TN))
            self_prob = jnp.exp(head_sums(qf * k_own) + closed_ref[at, :] - lse)
            self_slope = self_prob * (head_sums(backf * v_own) - delta)
            dko_ref[pair, at, :] = self_slope * qf
            dvo_ref[pair, at, :] = self_prob * backf
            dq_ref[pair, at, :] = ((dq + self_slope * k_own) * 0.125).astype(BF)
            return carried

        lax.fori_loop(0, q_ref.shape[0], one_pair, 0, unroll=UNROLL_BACKWARD)

    for_windows(meta, turn, rows, keys_all, one_tile)
    tiles = key_tiles(meta, turn)
    start = pl.multiple_of(meta[0] * rows, rows)
    own = pl.ds(start, rows)
    other = pl.ds(pl.multiple_of(rows - start, rows), rows)
    for count in range(1, keys_all // K_TILE + 1):

        @pl.when(tiles == count)
        def _():
            used = slice(0, count * K_TILE)
            for low_ref, packed_ref, self_ref in ((dkl_ref, dk_ref, dko_ref), (dvl_ref, dv_ref, dvo_ref)):
                packed = jnp.concatenate(
                    [packed_ref[i, used, :].astype(BF) for i in range(packed_ref.shape[0])], axis=1
                )
                low_ref[own, :] = (dot(sel_ref[used, own], packed, TN) + joined(self_ref)).astype(BF)
                low_ref[other, :] = dot(sel_ref[used, other], packed, TN).astype(BF)


def entry_slopes(meta, weights_ref, dq_ref, dkl_ref, dvl_ref, slope_own_ref, slope_oth_ref):
    half = weights_ref.shape[3]
    rows = dq_ref.shape[1]
    start = pl.multiple_of(meta[0] * rows, rows)

    def through(values, part):
        return dot(values[:, :half], weights_ref[0, part], NT) + dot(values[:, half:], weights_ref[1, part], NT)

    def from_keys(at):
        return through(dkl_ref[at, :], 1) + through(dvl_ref[at, :], 2)

    slope_own_ref[...] += through(joined(dq_ref), 0) + from_keys(pl.ds(start, rows))
    slope_oth_ref[...] = from_keys(pl.ds(pl.multiple_of(rows - start, rows), rows)).astype(BF)


class Moves:
    def __init__(self, sems):
        self.sems, self.used = sems, 0

    def start(self, source, target):
        copy = pltpu.make_async_copy(source, target, self.sems.at[self.used])
        self.used += 1
        copy.start()
        return copy


def wait(*copies):
    for copy in copies:
        copy.wait()


def rows_at(index, rows):
    return pl.ds(pl.multiple_of(index * rows, rows), rows)


def gather_entries(moves, meta, i, target):
    rows = i.entry_own.shape[0]
    return [
        moves.start(i.entry_own, target.at[rows_at(meta[0], rows), :]),
        moves.start(i.entry_oth, target.at[rows_at(1 - meta[0], rows), :]),
    ]


def fetch_heads_weights(moves, i, s):
    return [moves.start(i.own, s.weights.at[0]), moves.start(i.oth, s.weights.at[1])]


def fetch_feed_weights(moves, i, s):
    return [
        moves.start(source, target.at[side])
        for target, pair in ((s.comb, (i.comb0, i.comb1)), (s.exp_w, (i.exp0, i.exp1)), (s.red, (i.red0, i.red1)))
        for side, source in enumerate(pair)
    ]


def fetch(moves, i, s, *names):
    return [moves.start(getattr(i, name), getattr(s, name)) for name in names]


def as_row(square):
    return jnp.concatenate([square[r : r + 1, :] for r in range(square.shape[0])], axis=1)


def prepare(i, o, s):
    n_cells = i.lengths.shape[1]
    known = (i.known[...] > 0).astype(F32)
    chosen = (i.chosen[...] > 0).astype(F32)
    seen = jnp.maximum(known, chosen)
    block = known.shape[0]
    both = jnp.concatenate([known, seen], axis=0).astype(BF)
    row = lax.broadcasted_iota(jnp.int32, (PAIR, PAIR), 0)
    lane = lax.broadcasted_iota(jnp.int32, (PAIR, PAIR), 1)
    within = dot(both, (row < lane).astype(BF))
    totals = dot(both, jnp.ones((PAIR, PAIR), BF)).astype(BF)
    row = lax.broadcasted_iota(jnp.int32, (2 * block, 2 * block), 0)
    lane = lax.broadcasted_iota(jnp.int32, (2 * block, 2 * block), 1)
    earlier = ((lane < row) & ((lane < block) == (row < block))).astype(BF)
    places = jnp.where(both.astype(F32) > 0.5, within + dot(earlier, totals), -1.0)
    s.ranks[...] = jnp.concatenate(
        [as_row(places[:block]), as_row(places[block:]), jnp.zeros((6, s.ranks.shape[1]), F32)], axis=0
    )
    s.flags[...] = jnp.concatenate(
        [as_row(known), as_row(seen), as_row(chosen), jnp.zeros((13, s.flags.shape[1]), F32)], axis=0
    ).astype(BF)
    position = lax.broadcasted_iota(jnp.int32, known.shape, 0) * PAIR + lax.broadcasted_iota(jnp.int32, known.shape, 1)
    o.meta[0] = lax.axis_index("tensor").astype(jnp.int32)
    end = 0
    for c in range(n_cells):
        end = end + i.lengths[0, c]
        o.meta[1 + c] = end
        for turn, shown in enumerate((known, seen)):
            count = jnp.sum(jnp.where(position < end, shown, 0.0))
            o.meta[1 + n_cells * (1 + turn) + c] = count.astype(jnp.int32)
    s.vec[...] = jnp.concatenate(
        [
            *(ref[...].reshape(1, -1) for ref in (i.baseline, i.scales, i.shifts, i.adjustment, i.rescales, i.reshifts)),
            jnp.concatenate([i.thr0[...].astype(F32).reshape(1, -1), i.thr1[...].astype(F32).reshape(1, -1)], axis=1),
            jnp.concatenate([i.off0[...], i.off1[...]], axis=1),
            jnp.zeros((7, s.vec.shape[1]), F32),
        ],
        axis=0,
    )


def first_kernel(i, o, s):
    moves, meta = Moves(s.sems), o.meta
    rows = i.entry_own.shape[0]
    weights = fetch_heads_weights(moves, i, s)
    prepare(i, o, s)
    early = gather_entries(moves, meta, i, s.entry_all) + weights
    late = fetch_feed_weights(moves, i, s)
    saved = fetch(moves, s, o, "flags", "ranks", "vec")
    key_marks(meta, 0, s.marks)
    select_keys(meta, 0, s.ranks, s.sel)
    wait(*early)
    entry_own = s.entry_all[rows_at(meta[0], rows), :]
    project(meta, 0, entry_own, s.entry_all, s.weights, s.vec, s.sel, s.q, s.k, s.v, s.ko, s.vo)
    saved += fetch(moves, s, o, "q", "k", "v", "ko", "vo")
    attend(meta, 0, s.flags, s.q, s.k, s.v, s.ko, s.vo, s.marks, s.closed, s.off, s.top, s.edge, s.ctx, s.lse)
    saved += fetch(moves, s, o, "ctx", "lse")
    wait(*late)
    entry_own = s.entry_all[rows_at(meta[0], rows), :]
    result = feed_forward(entry_own, s.ctx, s.comb, s.exp_w, s.red, s.vec, s.before, s.unit1, s.unit2, s.rs)
    low = result.astype(BF)
    chosen = flag_column(meta, s.flags, 2, rows)[:, :1] > 0.5
    s.second[...] = jnp.where(chosen, low, entry_own)
    s.low[...] = low
    saved += fetch(moves, s, o, "second", "low", "before", "unit1", "unit2", "rs")
    wait(*saved)


def second_kernel(i, o, s):
    moves, meta = Moves(s.sems), i.meta
    rows = i.entry_own.shape[0]
    first = fetch(moves, i, s, "ranks", "flags", "vec")
    early = gather_entries(moves, meta, i, s.entry_all) + fetch_heads_weights(moves, i, s)
    late = fetch_feed_weights(moves, i, s) + fetch(moves, i, s, "cotangent")
    key_marks(meta, 1, s.marks)
    wait(*first)
    select_keys(meta, 1, s.ranks, s.sel)
    wait(*early)
    saved = fetch(moves, s, o, "entry_all")
    entry_own = s.entry_all[rows_at(meta[0], rows), :]
    project(meta, 1, entry_own, s.entry_all, s.weights, s.vec, s.sel, s.q, s.k, s.v, s.ko, s.vo)
    attend(meta, 1, s.flags, s.q, s.k, s.v, s.ko, s.vo, s.marks, s.closed, s.off, s.top, s.edge, s.ctx, s.lse)
    saved += fetch(moves, s, o, "ctx")
    wait(*late)
    entry_own = s.entry_all[rows_at(meta[0], rows), :]
    result = feed_forward(entry_own, s.ctx, s.comb, s.exp_w, s.red, s.vec, s.before, s.unit1, s.unit2, s.rs)
    s.low[...] = result.astype(BF)
    saved += fetch(moves, s, o, "low")
    mixture_slope, sums = feed_backward(s.cotangent[...].astype(F32), s.before, s.unit1, s.unit2, s.rs, s.comb, s.exp_w, s.red, s.vec, s.hid, s.sl, s.nl, s.bl, s.ml, s.do)
    s.sums[...] = padded(sums, s.sums)
    s.slope_own[...] = mixture_slope
    saved += fetch(moves, s, o, "hid", "sl", "nl", "bl", "ml", "sums")
    attend_backward(meta, 1, s.flags, s.q, s.k, s.v, s.ko, s.vo, s.marks, s.closed, s.ctx, s.lse, s.do, s.sel,
                    s.dq, s.dk, s.dv, s.dko, s.dvo, s.dkl, s.dvl)
    saved += fetch(moves, s, o, "dq", "dkl", "dvl")
    entry_slopes(meta, s.weights, s.dq, s.dkl, s.dvl, s.slope_own, s.slope_oth)
    saved += fetch(moves, s, o, "slope_oth", "slope_own")
    wait(*saved)


def padded(sums, like):
    return jnp.concatenate(sums + [jnp.zeros((like.shape[0] - len(sums), like.shape[1]), F32)], axis=0)


def side_by_side(matrix, rows):
    return jnp.concatenate([matrix[:rows], matrix[rows:]], axis=1)


def head_weights(meta, entry_all, dq_ref, dk, dv):
    rows = dq_ref.shape[1]
    dq = joined(dq_ref)
    parts = (dot(entry_all[rows_at(meta[0], rows), :], dq, TN), dot(entry_all[...], dk, TN), dot(entry_all[...], dv, TN))
    return parts, jnp.sum(dq.astype(F32), axis=0, keepdims=True), jnp.sum(dv.astype(F32), axis=0, keepdims=True)


def feed_weights(hid_ref, sl_ref, nl_ref, bl_ref, ctx_ref, ml_ref):
    return (
        dot(joined(ctx_ref), ml_ref[...], TN),
        dot(nl_ref[...], bl_ref[...], TN),
        dot(hid_ref[...], sl_ref[...], TN),
    )


def back_kernel(i, o, s):
    moves, meta = Moves(s.sems), i.meta
    first = fetch(moves, i, s, "flags", "cotangent", "slope_recv", "slope_own", "unit2", "rs")
    early = fetch(moves, i, s, "unit1", "vec", "before") + fetch_feed_weights(moves, i, s)
    next_ = fetch(moves, i, s, "ranks", "q", "ctx", "lse", "ko", "vo", "k", "v")
    late = fetch(moves, i, s, "sums2", "ctx2", "ml2", "nl2", "bl2", "hid2", "sl2")
    last = gather_entries(moves, meta, i, s.entry_all) + fetch_heads_weights(moves, i, s)
    last += fetch(moves, i, s, "entry2", "dq2", "dkl2", "dvl2")
    rows = i.slope_own.shape[0]
    half = i.comb0.shape[1] // 2
    key_marks(meta, 0, s.marks)
    wait(*first)
    chosen = flag_column(meta, s.flags, 2, rows)[:, :1] > 0.5
    second_slope = s.slope_own[...] + s.slope_recv[...].astype(F32)
    incoming = s.cotangent[...].astype(F32) + jnp.where(chosen, second_slope, 0.0)
    s.slope[...] = jnp.where(chosen, 0.0, second_slope)
    wait(*early)
    mixture_slope, sums = feed_backward(incoming, s.before, s.unit1, s.unit2, s.rs, s.comb, s.exp_w, s.red, s.vec, s.hid, s.sl, s.nl, s.bl, s.ml, s.do)
    s.slope[...] += mixture_slope
    s.sums[...] = padded(sums, s.sums)
    wait(*next_)
    select_keys(meta, 0, s.ranks, s.sel)
    attend_backward(meta, 0, s.flags, s.q, s.k, s.v, s.ko, s.vo, s.marks, s.closed, s.ctx, s.lse, s.do, s.sel,
                    s.dq, s.dk, s.dv, s.dko, s.dvo, s.dkl, s.dvl)
    wait(*late)
    for part, (left, right) in enumerate(zip(
        feed_weights(s.hid, s.sl, s.nl, s.bl, s.ctx, s.ml), feed_weights(s.hid2, s.sl2, s.nl2, s.bl2, s.ctx2, s.ml2)
    )):
        total = left + right
        for side, out in ((1, s.feed_oth), (0, s.feed_own)):
            mine = slice(side * half, (side + 1) * half)
            block = side_by_side(total[:, mine], half) if part == 1 else total[mine]
            out[part * half : (part + 1) * half] = block.astype(BF)
    saved = fetch(moves, s, o, "feed_oth", "feed_own")
    wait(*last)
    parts, q_sum, v_sum = head_weights(meta, s.entry_all, s.dq, s.dkl[...], s.dvl[...])
    parts2, q_sum2, v_sum2 = head_weights(meta, s.entry2, s.dq2, s.dkl2[...], s.dvl2[...])
    for c in range(3):
        total = parts[c] + parts2[c]
        for side, out in ((1, s.heads_oth), (0, s.heads_own)):
            cols = slice(side * half, (side + 1) * half)
            out[c * half : (c + 1) * half] = side_by_side(total[:, cols], half).astype(BF)
    s.sums[...] += s.sums2[...]
    s.sums[7:8, :] = q_sum + q_sum2
    s.sums[8:9, :] = v_sum + v_sum2
    saved += fetch(moves, s, o, "heads_oth", "heads_own", "sums")
    entry_slopes(meta, s.weights, s.dq, s.dkl, s.dvl, s.slope, s.slope_oth)
    saved += fetch(moves, s, o, "slope_oth", "slope")
    wait(*saved)


def call(kernel, micros, ins, outs, scratch):
    spaces = {"s": pltpu.SMEM, "v": pltpu.VMEM, "h": pl.ANY}
    scratch = scratch | {name: like for name, like in outs.items() if name != "meta"}
    in_names, out_names, scratch_names = list(ins), list(outs), list(scratch)

    def body(*refs):
        a, b = len(in_names), len(in_names) + len(out_names)
        kernel(
            types.SimpleNamespace(**dict(zip(in_names, refs[:a]))),
            types.SimpleNamespace(**dict(zip(out_names, refs[a:b]))),
            types.SimpleNamespace(sems=refs[-1], **dict(zip(scratch_names, refs[b:-1]))),
        )

    results = pl.pallas_call(
        body,
        out_shape=[jax.ShapeDtypeStruct(shape, kind) for shape, kind in outs.values()],
        in_specs=[pl.BlockSpec(memory_space=spaces[place]) for _, place in ins.values()],
        out_specs=[pl.BlockSpec(memory_space=pltpu.SMEM if name == "meta" else pl.ANY) for name in outs],
        scratch_shapes=[pltpu.VMEM(shape, kind) for shape, kind in scratch.values()] + [pltpu.SemaphoreType.DMA((48,))],
        compiler_params=pltpu.CompilerParams(vmem_limit_bytes=LIMITS[kernel.__name__] * 2**20),
        cost_estimate=pl.CostEstimate(flops=int(micros * 1.1e9), bytes_accessed=0, transcendentals=0),
    )(*[array for array, _ in ins.values()])
    return dict(zip(out_names, results))


def partner(value):
    return lax.ppermute(value, "tensor", [(0, 1), (1, 0)])


def flip(value, size, step):
    return lax.ppermute(value, "dp", [(i, i ^ step) for i in range(size)])


def tree_sum(parts):
    parts = list(parts)
    while len(parts) > 1:
        parts = [parts[i] + parts[i + 1] for i in range(0, len(parts), 2)]
    return parts[0]


def digits(size):
    out, stride = [], 1
    while stride < size:
        radix = 4 if size % (stride * 4) == 0 else 2
        out.append((stride, radix))
        stride *= radix
    return out


def sum_small(value, size):
    for stride, radix in digits(size):
        parts = [value] + [flip(value, size, k * stride) for k in range(1, radix)]
        value = tree_sum(parts)
    return value


def sum_large(value, size):
    me = lax.axis_index("dp")
    rows, width = value.shape
    order = jnp.arange(size, dtype=jnp.int32) ^ me
    value = jnp.take(value.reshape(size, rows // size, width), order, axis=0)
    shape = [radix for _, radix in digits(size)]
    value = value.reshape(shape[::-1] + [rows // size, width])
    n = len(shape)
    steps = range(n)
    for step in steps:
        stride, radix = digits(size)[step]
        axis = n - 1 - step
        take = lambda k: lax.index_in_dim(value, k, axis, keepdims=True)
        parts = [take(0).astype(F32)] + [flip(take(k), size, k * stride).astype(F32) for k in range(1, radix)]
        value = tree_sum(parts).astype(BF)
    for step in reversed(steps):
        stride, radix = digits(size)[step]
        axis = n - 1 - step
        value = jnp.concatenate([value] + [flip(value, size, k * stride) for k in range(1, radix)], axis=axis)
    value = value.reshape(size, rows // size, width)
    return jnp.take(value, order, axis=0).reshape(rows, width)


QUAD = 4


def target_of(place, first, second):
    return place[0] ^ jnp.where(place[1] == 0, second * QUAD + first, first * QUAD + second)


def spread_kernel(place, ins, out, s):
    feed_own, feed_recv, heads_own, heads_recv, vec_own, vec_recv = ins
    chunk = feed_own.shape[0] // QUAD**2
    half = vec_own.shape[1] // 2
    own, recv = vec_own[...], vec_recv[...]
    own_side = own[6:9, :half] + recv[6:9, half:]
    s.vec[...] = jnp.concatenate(
        [own[:6] + recv[:6], jnp.concatenate([own_side, jnp.zeros_like(own_side)], axis=1), jnp.zeros_like(own[9:])], axis=0
    )
    for first in range(QUAD):
        for second in range(QUAD):
            target = target_of(place, first, second)
            at = pl.ds(pl.multiple_of(target * chunk, 16), chunk)
            for n, (left, right) in enumerate(((feed_own, feed_recv), (heads_own, heads_recv))):
                total = left[at, :].astype(F32) + right[at, :].astype(F32)
                out[first][second, chunk * n : chunk * (n + 1), :] = total.astype(BF)
            row = s.vec[pl.ds(target, 1), :]
            out[first][second, 2 * chunk :, :] = jnp.broadcast_to(row, (8, row.shape[1])).astype(BF)


def added(refs, *index):
    parts = [ref[index].astype(F32) for ref in refs]
    return ((parts[0] + parts[1]) + (parts[2] + parts[3])).astype(BF)


def between_kernel(got, out):
    for k in range(QUAD):
        out[k][...] = added(got, k)


def ended_kernel(got, out):
    out[0][...] = added(got)


def stack_kernel(got, out):
    for k in range(QUAD):
        out[0][k] = got[k][...]


def unfold(matrix):
    half = matrix.shape[1] // 2
    return jnp.concatenate([matrix[:, :half], matrix[:, half:]], axis=0)


def collect_kernel(place, got, out, s):
    chunk = s.feed.shape[0] // QUAD**2
    rows = s.feed.shape[0] // 3
    for first in range(QUAD):
        for second in range(QUAD):
            target = target_of(place, first, second)
            at = pl.ds(pl.multiple_of(target * chunk, 16), chunk)
            for n, into in enumerate((s.feed, s.heads)):
                into[at, :] = got[first][second, chunk * n : chunk * (n + 1), :].astype(F32)
            s.vec[pl.ds(target, 1), :] = got[first][second, 2 * chunk : 2 * chunk + 1, :].astype(F32)
    for c in range(3):
        out.heads[c] = unfold(s.heads[c * rows : (c + 1) * rows, :])
    out.comb[...] = s.feed[:rows, :]
    out.exp_w[...] = unfold(s.feed[rows : 2 * rows, :])
    out.red[...] = s.feed[2 * rows :, :]
    out.vec[...] = s.vec[:8, :]
    out.thr[...] = s.vec[6:7, : s.vec.shape[1] // 2]
    out.off[...] = s.vec[7:9, : s.vec.shape[1] // 2]


def plain_call(body, args, outs, scratch=()):
    return pl.pallas_call(
        body,
        out_shape=[jax.ShapeDtypeStruct(shape, kind) for shape, kind in outs],
        in_specs=[pl.BlockSpec(memory_space=pltpu.SMEM if a.dtype == jnp.int32 else pltpu.VMEM) for a in args],
        out_specs=[pl.BlockSpec(memory_space=pltpu.VMEM)] * len(outs),
        scratch_shapes=list(scratch),
        compiler_params=pltpu.CompilerParams(vmem_limit_bytes=LIMITS["small"] * 2**20),
    )(*args)


def sum_quads(size, feed, heads, vec):
    rows, width = feed[0].shape
    half = width // 2
    side = lax.axis_index("tensor").astype(jnp.int32)
    place = jnp.stack([lax.axis_index("dp").astype(jnp.int32), side])
    tall = 2 * (rows // QUAD**2) + 8
    quarter = ((QUAD, tall, width), BF)
    operands = [*feed, *heads, *vec]

    def spread_body(*refs):
        spread_kernel(refs[0], refs[1:7], refs[7:11], types.SimpleNamespace(vec=refs[11]))

    def four(kernel):
        return lambda *refs: kernel(refs[:QUAD], refs[QUAD:])

    def exchange(parts, steps):
        got = [parts[0]]
        for k in range(1, QUAD):
            perm = [(2 * n + core, 2 * (n ^ (k * steps[core])) + core) for n in range(size) for core in range(2)]
            got.append(lax.ppermute(parts[k], ("dp", "tensor"), perm))
        return got

    vmem = lambda like: pltpu.VMEM(*like)
    parts = plain_call(
        spread_body,
        [place, *operands],
        [quarter] * QUAD,
        [vmem(((16, width), F32))],
    )
    parts = plain_call(four(between_kernel), exchange(parts, (1, QUAD)), [((tall, width), BF)] * QUAD)
    (total,) = plain_call(four(ended_kernel), exchange(parts, (QUAD, 1)), [((tall, width), BF)])
    (total,) = plain_call(four(stack_kernel), exchange([total] * QUAD, (QUAD, 1)), [quarter])
    got = exchange([total] * QUAD, (1, QUAD))

    def collect_body(*refs):
        outs = types.SimpleNamespace(**dict(zip(("heads", "comb", "exp_w", "red", "off", "thr", "vec"), refs[5:12])))
        scratch = types.SimpleNamespace(feed=refs[12], heads=refs[13], vec=refs[14])
        collect_kernel(refs[0], refs[1:5], outs, scratch)

    *totals, vectors = plain_call(
        collect_body,
        [place, *got],
        [((3, width, half), F32), ((half, width), F32), ((width, half), F32), ((half, width), F32), ((2, half), F32), ((1, half), F32), ((8, width), F32)],
        [vmem(((rows, width), F32)), vmem(((rows, width), F32)), vmem(((16, width), F32))],
    )
    vectors = jnp.where(side == 0, vectors, partner(vectors))
    return (*totals, *(vectors[n] for n in range(6)))


def sum_any(size, feed, heads, vec):
    half = feed[0].shape[1] // 2
    width = 2 * half
    total = lambda pair: sum_large((pair[0].astype(F32) + pair[1].astype(F32)).astype(BF), size).astype(F32)
    feed, heads = total(feed), total(heads).reshape(3, half, width)
    own, recv = vec
    sides = jnp.pad(own[6:9, :half] + recv[6:9, half:], ((0, 0), (0, half)))
    vec = sum_small(jnp.concatenate([own[:6] + recv[:6], sides], axis=0), size)
    return (
        jnp.stack([unfold(heads[c]) for c in range(3)]), feed[:half], unfold(feed[half : 2 * half]), feed[2 * half :],
        vec[7:9, :half], vec[6:7, :half], *(vec[c : c + 1] for c in range(6)),
    )


def on_device(dp, tokens, first_cotangent, second_cotangent, projection, offsets, combiner, baseline, scales, shifts,
              expander, thresholds, reducer, adjustment, rescales, reshifts, known_flags, chosen_flags, cell_lengths):
    rows, width = tokens.shape
    group = known_flags.shape[0]
    half = projection.shape[2]
    pairs = 2 * half // PAIR
    n_cells = cell_lengths.shape[1]
    entry_oth, oth, comb1, exp1, red1, offsets_oth, thresholds_oth = (
        partner(v) for v in (tokens, projection, combiner, expander, reducer, offsets, thresholds)
    )
    small_in = {
        "lengths": (cell_lengths, "s"), "known": (known_flags.reshape(-1, PAIR), "v"), "chosen": (chosen_flags.reshape(-1, PAIR), "v"),
        "baseline": (baseline, "v"), "scales": (scales, "v"), "shifts": (shifts, "v"), "adjustment": (adjustment, "v"),
        "rescales": (rescales, "v"), "reshifts": (reshifts, "v"), "thr0": (thresholds, "v"), "thr1": (thresholds_oth, "v"), "off0": (offsets, "v"), "off1": (offsets_oth, "v"),
    }
    square, square32 = ((rows, width), BF), ((rows, width), F32)
    spread = ((rows, PAIR), F32)
    own_pairs, own_pairs32 = ((pairs, rows, PAIR), BF), ((pairs, rows, PAIR), F32)
    all_pairs, all_pairs32 = ((pairs, group, PAIR), BF), ((pairs, group, PAIR), F32)
    entries, grads_like, sums_like = ((group, width), BF), ((3 * half, width), BF), ((16, width), F32)
    square3 = ((3, width, width), F32)
    comb_like, exp_like = ((2,) + combiner.shape, BF), ((2,) + expander.shape, BF)
    weights_like = {"weights": ((2,) + projection.shape, BF), "comb": comb_like, "exp_w": exp_like, "red": comb_like}
    state_like = {
        "entry_all": entries, "sel": ((group, group), BF), "marks": ((group, PAIR), BF), "q": own_pairs, "k": all_pairs, "v": all_pairs,
        "ko": own_pairs, "vo": own_pairs, "ctx": own_pairs, "lse": own_pairs32, "before": square32, "unit1": square32, "unit2": square32, "rs": spread,
    }
    made_like = {"hid": square, "sl": square, "nl": square, "bl": square, "ml": square}
    back_scratch = {"closed": spread, "dk": all_pairs32, "dv": all_pairs32, "dko": own_pairs32, "dvo": own_pairs32}
    slopes_like = {"dq": own_pairs, "dkl": entries, "dvl": entries}
    saved_names = tuple(name for name in state_like if name not in ("entry_all", "sel", "marks"))
    heads_names = ("q", "k", "v", "ko", "vo", "lse", "ctx")
    norm_names = ("before", "unit1", "unit2", "rs")
    closed = {
        "closed": spread, "off": own_pairs32, "top": ((pairs, rows // Q_TILE, 2 * Q_TILE, PAIR), F32), "edge": ((2, 8, PAIR), F32),
    }
    likes = lambda names: {name: state_like[name] for name in names}
    feed_like = {name: weights_like[name] for name in ("comb", "exp_w", "red")}
    small_like = {"flags": ((16, group), BF), "ranks": ((8, group), F32), "vec": sums_like}
    heads_in = {"own": (projection, "h"), "oth": (oth, "h")}
    feed_in = {name: (array, "h") for name, array in (
        ("comb0", combiner), ("comb1", comb1), ("exp0", expander), ("exp1", exp1), ("red0", reducer), ("red1", red1))}
    held = lambda values, *names: {name: (values[name], "h") for name in names}

    one = call(
        first_kernel, 13,
        small_in | {"entry_own": (tokens, "h"), "entry_oth": (entry_oth, "h")} | heads_in | feed_in,
        {"meta": ((1 + 3 * n_cells,), jnp.int32), "low": square, "second": square} | small_like | likes(saved_names),
        closed | weights_like | likes(("entry_all", "sel", "marks")),
    )
    second_oth = partner(one["second"])
    table = {"meta": (one["meta"], "s")} | held(one, *small_like)
    two = call(
        second_kernel, 28,
        table | {"entry_own": (one["second"], "h"), "entry_oth": (second_oth, "h"), "cotangent": (second_cotangent, "h")} | heads_in | feed_in,
        {"low": square, "slope_oth": square, "slope_own": square32, "sums": sums_like} | likes(("entry_all", "ctx")) | made_like | slopes_like,
        closed | small_like | weights_like | state_like | back_scratch | {"cotangent": square, "do": own_pairs},
    )
    slope_recv = partner(two["slope_oth"])
    kept_names = tuple(made_like) + ("ctx", "sums") + tuple(slopes_like)
    kept_like = {name + "2": (made_like | slopes_like | {"ctx": own_pairs, "sums": sums_like})[name] for name in kept_names}
    last = call(
        back_kernel, 25,
        table | heads_in | feed_in
        | {"entry_own": (tokens, "h"), "entry_oth": (entry_oth, "h"), "cotangent": (first_cotangent, "h"), "slope_recv": (slope_recv, "h")}
        | held(one, *heads_names, *norm_names) | held(two, "slope_own")
        | {name + "2": (two[name], "h") for name in kept_names} | {"entry2": (two["entry_all"], "h")},
        {"slope": square32, "slope_oth": square, "sums": sums_like, "feed_own": grads_like, "feed_oth": grads_like, "heads_own": grads_like, "heads_oth": grads_like},
        small_like | weights_like | made_like | kept_like | slopes_like | state_like | back_scratch
        | {"entry2": entries, "cotangent": square, "slope_recv": square, "slope_own": square32, "do": own_pairs},
    )
    tokens_gradient = last["slope"] + partner(last["slope_oth"]).astype(F32)
    summed = (sum_quads if dp == QUAD**2 else sum_any)(
        dp,
        (last["feed_own"], partner(last["feed_oth"])),
        (last["heads_own"], partner(last["heads_oth"])),
        (last["sums"], partner(last["sums"])),
    )
    heads_total, comb_total, exp_total, red_total, off_total, thr_total, *vectors = summed
    base_total, scale_total, shift_total, adjust_total, rescale_total, reshift_total = (v.reshape(-1) for v in vectors)
    return (
        one["low"],
        two["low"],
        tokens_gradient,
        heads_total,
        off_total,
        comb_total,
        base_total,
        scale_total,
        shift_total,
        exp_total,
        thr_total.reshape(-1),
        red_total,
        adjust_total,
        rescale_total,
        reshift_total,
    )


def solution(mesh):
    rows = P(("dp", "tensor"), None)
    return jax.shard_map(
        functools.partial(on_device, mesh.shape["dp"]),
        mesh=mesh,
        in_specs=(
            rows, rows, rows, P(None, None, "tensor"), P(None, "tensor"), P("tensor", None), P(), P(), P(),
            P(None, "tensor"), P("tensor"), P("tensor", None), P(), P(), P(), P("dp"), P("dp"), P("dp", None),
        ),
        out_specs=(
            rows, rows, rows, P(None, None, "tensor"), P(None, "tensor"), P("tensor", None), P(), P(), P(),
            P(None, "tensor"), P("tensor"), P("tensor", None), P(), P(), P(),
        ),
        check_vma=False,
    )
```

```python
import functools
import types

import jax
import jax.numpy as jnp
from jax import lax
from jax.experimental import pallas as pl
from jax.experimental.pallas import tpu as pltpu
from jax.sharding import PartitionSpec as P

HD = 64
PAIR = 2 * HD
BF = jnp.bfloat16
F32 = jnp.float32
HIDE = -1e30
SAFE = 60.0
LEAST = 1e-26
NN = (((1,), (0,)), ((), ()))
NT = (((1,), (1,)), ((), ()))
TN = (((0,), (0,)), ((), ()))
LIMITS = {"first_kernel": 58, "second_kernel": 58, "back_kernel": 58, "small": 24}
UNROLL_FORWARD = 2
UNROLL_BACKWARD = 1
Q_TILE = 256
K_TILE = 256
WINDOWS = (128, 256, 384, 512, 640)


def dot(left, right, dims=NN):
    return lax.dot_general(left, right, dims, preferred_element_type=F32)


def lanes_of(rows):
    return lax.broadcasted_iota(jnp.int32, (rows, PAIR), 1)


def cells_of(meta):
    return (meta.shape[0] - 1) // 3


def row_cells(start, rows, meta, bounds):
    position = start + lax.broadcasted_iota(jnp.int32, (rows, PAIR), 0)
    cell = jnp.zeros((rows, PAIR), jnp.int32)
    for c in bounds:
        cell = cell + (position >= meta[c]).astype(jnp.int32)
    return cell


def norm_forward(values, gain, shift):
    centered = values - jnp.mean(values, axis=-1, keepdims=True)
    inverse = lax.rsqrt(jnp.mean(centered * centered, axis=-1, keepdims=True) + 1e-05)
    unit = centered * inverse
    return unit * gain + shift, unit, inverse


def norm_backward(gradient, unit, inverse, gain):
    scaled = gradient * gain
    projected = (
        scaled
        - jnp.mean(scaled, axis=-1, keepdims=True)
        - unit * jnp.mean(scaled * unit, axis=-1, keepdims=True)
    )
    return (
        projected * inverse,
        jnp.sum(gradient * unit, axis=0, keepdims=True),
        jnp.sum(gradient, axis=0, keepdims=True),
    )


def key_marks(meta, turn, marks_ref):
    rows = marks_ref.shape[0]
    n_cells = cells_of(meta)
    lane = lanes_of(rows)
    first = 1 + n_cells * (1 + turn)
    cell = row_cells(0, rows, meta, range(first, first + n_cells))
    marks_ref[...] = jnp.where(
        lane < n_cells,
        jnp.where(cell == lane, 0.0, HIDE),
        jnp.where((lane % HD >= n_cells) & (lane % HD < n_cells + 3), -1.0, 0.0),
    ).astype(BF)


def flag_column(meta, flags, row, rows):
    pick = (lax.broadcasted_iota(jnp.int32, (flags.shape[0], PAIR), 0) == row).astype(BF)
    start = pl.multiple_of(meta[0] * rows, rows)
    return dot(flags[:, pl.ds(start, rows)], pick, TN)


def key_tiles(meta, turn):
    count = meta[n_bounds(meta, turn)]
    return jnp.maximum((count + K_TILE - 1) // K_TILE, 1)


def n_bounds(meta, turn):
    return cells_of(meta) * (2 + turn)


def select_keys(meta, turn, ranks, sel_ref):
    keys_all = ranks.shape[1]
    tiles = key_tiles(meta, turn)
    place = ranks[turn : turn + 1, :]
    for tile in range(keys_all // K_TILE):

        @pl.when(tile < tiles)
        def _():
            row = (lax.broadcasted_iota(jnp.int32, (K_TILE, keys_all), 0) + tile * K_TILE).astype(F32)
            sel_ref[tile * K_TILE : (tile + 1) * K_TILE, :] = (row == place).astype(BF)


def spread_pairs(ref, side, half, at, values):
    for part in range(half // PAIR):
        ref[side * (half // PAIR) + part, at, :] = values[:, part * PAIR : (part + 1) * PAIR]


def project(meta, turn, entry_own, entry_all, weights_ref, vec, sel_ref, q_ref, k_ref, v_ref, ko_ref, vo_ref):
    half = weights_ref.shape[3]
    every = slice(None)
    for side in range(2):
        cols = slice(side * half, (side + 1) * half)
        queries = (dot(entry_own, weights_ref[side, 0]) + vec[7:8, cols]).astype(BF) * 0.125
        spread_pairs(q_ref, side, half, every, queries.astype(BF))
        spread_pairs(ko_ref, side, half, every, dot(entry_own, weights_ref[side, 1]).astype(BF))
        spread_pairs(vo_ref, side, half, every, (dot(entry_own, weights_ref[side, 2]) + vec[8:9, cols]).astype(BF))
    tiles = key_tiles(meta, turn)
    for tile in range(entry_all.shape[0] // K_TILE):
        at = slice(tile * K_TILE, (tile + 1) * K_TILE)

        @pl.when(tile < tiles)
        def _():
            entry = dot(sel_ref[at, :], entry_all[...]).astype(BF)
            for side in range(2):
                cols = slice(side * half, (side + 1) * half)
                spread_pairs(k_ref, side, half, at, dot(entry, weights_ref[side, 1]).astype(BF))
                spread_pairs(v_ref, side, half, at, (dot(entry, weights_ref[side, 2]) + vec[8:9, cols]).astype(BF))

        @pl.when(tile >= tiles)
        def _():
            k_ref[:, at, :] = jnp.zeros((k_ref.shape[0], K_TILE, PAIR), BF)
            v_ref[:, at, :] = jnp.zeros((v_ref.shape[0], K_TILE, PAIR), BF)


def for_windows(meta, turn, rows, keys_all, body):
    n_cells = cells_of(meta)
    ends, seen = 1, 1 + n_cells * (1 + turn)

    def one_tile(tile, carried):
        first = meta[0] * rows + tile * Q_TILE
        last = first + Q_TILE - 1
        low, high = 0, meta[seen + n_cells - 1]
        for c in range(n_cells - 1):
            low = jnp.where(first >= meta[ends + c], meta[seen + c], low)
            d = n_cells - 2 - c
            high = jnp.where(last < meta[ends + d], meta[seen + d], high)
        low = (low // 16) * 16
        need = high - low
        below = -1
        for width in WINDOWS + (keys_all,):
            start = pl.multiple_of(jnp.minimum(low, keys_all - width), 16)

            @pl.when((need > below) & (need <= width))
            def _():
                body(tile, start, width)

            below = width
        return carried

    lax.fori_loop(0, rows // Q_TILE, one_tile, 0)


def head_sums(values):
    high = values.astype(BF)
    low = (values - high.astype(F32)).astype(BF)
    row = lax.broadcasted_iota(jnp.int32, (2 * PAIR, PAIR), 0) % PAIR
    lane = lax.broadcasted_iota(jnp.int32, (2 * PAIR, PAIR), 1)
    ones = ((row < HD) == (lane < HD)).astype(BF)
    return dot(jnp.concatenate([high, low], axis=1), ones)


def by_head(values):
    lane = lax.broadcasted_iota(jnp.int32, values.shape, 1)
    zero = jnp.zeros_like(values)
    return jnp.concatenate([jnp.where(lane < HD, values, zero), jnp.where(lane < HD, zero, values)], axis=0)


def merge_heads(values):
    rows = values.shape[0] // 2
    lane = lanes_of(rows)
    return jnp.where(lane < HD, values[:rows], values[rows:])


def own_places(meta, first, rows):
    n_cells = cells_of(meta)
    lane = lanes_of(rows)
    cell = row_cells(first, rows, meta, range(1, n_cells))
    return jnp.where((cell == lane) & (lane < n_cells), 1.0, 0.0)


def row_tails(place, offset, n_cells):
    lane = lanes_of(offset.shape[0])
    side = lane % HD
    high = offset.astype(BF).astype(F32)
    middle = (offset - high).astype(BF).astype(F32)
    taken = jnp.where(
        side == n_cells,
        high,
        jnp.where(side == n_cells + 1, middle, jnp.where(side == n_cells + 2, offset - high - middle, 0.0)),
    )
    return jnp.concatenate(
        [jnp.where(lane < HD, taken, 0.0) + place, jnp.where(lane < HD, 0.0, taken) + place], axis=0
    ).astype(BF)


def attend(meta, turn, flags, q_ref, k_ref, v_ref, ko_ref, vo_ref, marks_ref, closed_ref, off_ref, top_ref, edge_ref, ctx_ref, lse_ref):
    pairs, rows = q_ref.shape[0], q_ref.shape[1]
    n_cells = cells_of(meta)
    lane = lanes_of(Q_TILE)
    closed_ref[...] = jnp.where(flag_column(meta, flags, turn, rows) > 0.5, HIDE, 0.0)
    off_ref[...] = jnp.zeros_like(off_ref)

    def own_scores(pair, at):
        product = q_ref[pair, at, :].astype(F32) * ko_ref[pair, at, :].astype(F32)
        return head_sums(product) + closed_ref[at, :] - off_ref[pair, at, :]

    def one_tile(tile, start, width):
        at = pl.ds(pl.multiple_of(tile * Q_TILE, Q_TILE), Q_TILE)
        place = own_places(meta, meta[0] * rows + tile * Q_TILE, Q_TILE)
        window = pl.ds(start, width)

        def one_pair(pair, carried):
            offset = off_ref[pair, at, :]
            keys = jnp.concatenate([k_ref[pair, window, :], marks_ref[window, :]], axis=1)
            vals = jnp.concatenate([v_ref[pair, window, :], jnp.ones((width, PAIR), BF)], axis=1)
            asked = jnp.concatenate([by_head(q_ref[pair, at, :]), row_tails(place, offset, n_cells)], axis=1)
            scores = dot(asked, keys, NT)
            mixed = dot(jnp.exp(scores).astype(BF), vals)
            top = scores[:, :PAIR]
            for part in range(1, width // PAIR):
                top = jnp.maximum(top, scores[:, part * PAIR : (part + 1) * PAIR])
            top_ref[pair, tile] = top
            self_score = own_scores(pair, at)
            self_weight = jnp.exp(self_score)
            total = merge_heads(mixed[:, PAIR:]) + self_weight
            context = (merge_heads(mixed[:, :PAIR]) + self_weight * vo_ref[pair, at, :].astype(F32)) / total
            ctx_ref[pair, at, :] = context.astype(BF)
            lse_ref[pair, at, :] = offset + jnp.log(total)
            highest = jnp.maximum(jnp.maximum(top[:Q_TILE], top[Q_TILE:]), self_score)
            edge_ref[0] = jnp.maximum(edge_ref[0], jnp.max(highest.reshape(-1, 8, PAIR), axis=0))
            edge_ref[1] = jnp.minimum(edge_ref[1], jnp.min(total.reshape(-1, 8, PAIR), axis=0))
            return carried

        lax.fori_loop(0, pairs, one_pair, 0, unroll=UNROLL_FORWARD)

    def attempt(_):
        edge_ref[0] = jnp.full(edge_ref.shape[1:], HIDE, F32)
        edge_ref[1] = jnp.ones(edge_ref.shape[1:], F32)
        for_windows(meta, turn, rows, k_ref.shape[1], one_tile)
        again = (jnp.max(edge_ref[0]) > SAFE) | (jnp.min(edge_ref[1]) < LEAST)

        @pl.when(again)
        def _():
            def raise_pair(index, carried):
                tile, pair = index // pairs, index % pairs
                at = pl.ds(pl.multiple_of(tile * Q_TILE, Q_TILE), Q_TILE)
                top = jnp.max(top_ref[pair, tile], axis=1, keepdims=True)
                tops = jnp.where(lane < HD, top[:Q_TILE], top[Q_TILE:])
                off_ref[pair, at, :] = off_ref[pair, at, :] + jnp.maximum(tops, own_scores(pair, at))
                return carried

            lax.fori_loop(0, pairs * (rows // Q_TILE), raise_pair, 0)

        return again.astype(jnp.int32)

    lax.while_loop(lambda again: again > 0, attempt, jnp.int32(1))


def joined(ref):
    return jnp.concatenate([ref[i] for i in range(ref.shape[0])], axis=1)


def feed_forward(entry_own, ctx_ref, comb, exp_w, red, vec, before_ref, unit1_ref, unit2_ref, rs_ref):
    context = joined(ctx_ref)
    half = comb.shape[1]
    attended = dot(context[:, :half], comb[0]) + dot(context[:, half:], comb[1])
    mixture = entry_own.astype(F32) + attended + vec[0:1, :]
    normed, unit1, inverse1 = norm_forward(mixture, vec[1:2, :], vec[2:3, :])
    unit1_ref[...] = unit1
    normed_low = normed.astype(BF)
    summed = normed + vec[3:4, :]
    for side in range(2):
        cols = slice(side * half, (side + 1) * half)
        before = dot(normed_low, exp_w[side]) + vec[6:7, cols]
        before_ref[:, cols] = before
        hidden = (0.5 * before * (1.0 + lax.erf(before * 0.7071067811865476))).astype(BF)
        summed = summed + dot(hidden, red[side])
    result, unit2, inverse2 = norm_forward(summed, vec[4:5, :], vec[5:6, :])
    unit2_ref[...] = unit2
    rows = result.shape[0]
    rs_ref[...] = jnp.where(lanes_of(rows) < HD, inverse1, inverse2)
    return result


def feed_backward(incoming, before_ref, unit1_ref, unit2_ref, rs_ref, comb, exp_w, red, vec, hid_ref, sl_ref, nl_ref, bl_ref, ml_ref, do_ref):
    half = comb.shape[1]
    inverse1 = rs_ref[:, :1]
    inverse2 = rs_ref[:, PAIR - 1 :]
    summed_slope, rescale_part, reshift_part = norm_backward(
        incoming, unit2_ref[...], inverse2, vec[4:5, :]
    )
    summed_low = summed_slope.astype(BF)
    sl_ref[...] = summed_low
    unit1 = unit1_ref[...]
    nl_ref[...] = (unit1 * vec[1:2, :] + vec[2:3, :]).astype(BF)
    normed_slope = summed_slope
    threshold_parts = []
    for side in range(2):
        cols = slice(side * half, (side + 1) * half)
        before = before_ref[:, cols]
        phi = 0.5 * (1.0 + lax.erf(before * 0.7071067811865476))
        hid_ref[:, cols] = (before * phi).astype(BF)
        slope = phi + before * jnp.exp(-0.5 * before * before) * 0.3989422804014327
        before_low = (dot(summed_low, red[side], NT) * slope).astype(BF)
        bl_ref[:, cols] = before_low
        threshold_parts.append(jnp.sum(before_low.astype(F32), axis=0, keepdims=True))
        normed_slope = normed_slope + dot(before_low, exp_w[side], NT)
    mixture_slope, scales_part, shifts_part = norm_backward(
        normed_slope, unit1, inverse1, vec[1:2, :]
    )
    mixture_low = mixture_slope.astype(BF)
    ml_ref[...] = mixture_low
    for side in range(2):
        back = dot(mixture_low, comb[side], NT).astype(BF)
        for part in range(half // PAIR):
            do_ref[side * (half // PAIR) + part] = back[:, part * PAIR : (part + 1) * PAIR]
    sums = [
        jnp.sum(mixture_slope, axis=0, keepdims=True),
        scales_part,
        shifts_part,
        jnp.sum(summed_slope, axis=0, keepdims=True),
        rescale_part,
        reshift_part,
        jnp.concatenate(threshold_parts, axis=1),
    ]
    return mixture_slope, sums


def attend_backward(meta, turn, flags, q_ref, k_ref, v_ref, ko_ref, vo_ref, marks_ref, closed_ref, ctx_ref, lse_ref, do_ref, sel_ref,
                    dq_ref, dk_ref, dv_ref, dko_ref, dvo_ref, dkl_ref, dvl_ref):
    rows = q_ref.shape[1]
    n_cells = cells_of(meta)
    keys_all = k_ref.shape[1]
    lane = lanes_of(Q_TILE)
    closed_ref[...] = jnp.where(flag_column(meta, flags, turn, rows) > 0.5, HIDE, 0.0)
    dk_ref[...] = jnp.zeros_like(dk_ref)
    dv_ref[...] = jnp.zeros_like(dv_ref)

    def one_tile(tile, start, width):
        at = pl.ds(pl.multiple_of(tile * Q_TILE, Q_TILE), Q_TILE)
        place = own_places(meta, meta[0] * rows + tile * Q_TILE, Q_TILE)
        side = lane % HD
        window = pl.ds(start, width)
        def one_pair(pair, carried):
            q, back = q_ref[pair, at, :], do_ref[pair, at, :]
            qf, backf = q.astype(F32), back.astype(F32)
            k_own, v_own = ko_ref[pair, at, :].astype(F32), vo_ref[pair, at, :].astype(F32)
            k_pair = k_ref[pair, window, :]
            keys = jnp.concatenate([k_pair, marks_ref[window, :]], axis=1)
            vals = jnp.concatenate([v_ref[pair, window, :], jnp.ones((width, PAIR), BF)], axis=1)
            lse = lse_ref[pair, at, :]
            tails = row_tails(place, lse, n_cells)
            delta = head_sums(backf * ctx_ref[pair, at, :].astype(F32))
            high = delta.astype(BF).astype(F32)
            marks = jnp.where(side == 0, -high, jnp.where(side == 1, high - delta, 0.0)).astype(BF)
            q_two, back_two = by_head(q), by_head(back)
            probs = jnp.exp(dot(keys, jnp.concatenate([q_two, tails], axis=1), NT))
            slopes = dot(vals, jnp.concatenate([back_two, by_head(marks)], axis=1), NT)
            score_slope = (probs * slopes).astype(BF)
            dv_ref[pair, window, :] += dot(probs.astype(BF), back_two)
            dk_ref[pair, window, :] += dot(score_slope, q_two)
            dq = merge_heads(dot(score_slope, k_pair, TN))
            self_prob = jnp.exp(head_sums(qf * k_own) + closed_ref[at, :] - lse)
            self_slope = self_prob * (head_sums(backf * v_own) - delta)
            dko_ref[pair, at, :] = self_slope * qf
            dvo_ref[pair, at, :] = self_prob * backf
            dq_ref[pair, at, :] = ((dq + self_slope * k_own) * 0.125).astype(BF)
            return carried

        lax.fori_loop(0, q_ref.shape[0], one_pair, 0, unroll=UNROLL_BACKWARD)

    for_windows(meta, turn, rows, keys_all, one_tile)
    tiles = key_tiles(meta, turn)
    start = pl.multiple_of(meta[0] * rows, rows)
    own = pl.ds(start, rows)
    other = pl.ds(pl.multiple_of(rows - start, rows), rows)
    for count in range(1, keys_all // K_TILE + 1):

        @pl.when(tiles == count)
        def _():
            used = slice(0, count * K_TILE)
            for low_ref, packed_ref, self_ref in ((dkl_ref, dk_ref, dko_ref), (dvl_ref, dv_ref, dvo_ref)):
                packed = jnp.concatenate(
                    [packed_ref[i, used, :].astype(BF) for i in range(packed_ref.shape[0])], axis=1
                )
                low_ref[own, :] = (dot(sel_ref[used, own], packed, TN) + joined(self_ref)).astype(BF)
                low_ref[other, :] = dot(sel_ref[used, other], packed, TN).astype(BF)


def entry_slopes(meta, weights_ref, dq_ref, dkl_ref, dvl_ref, slope_own_ref, slope_oth_ref):
    half = weights_ref.shape[3]
    rows = dq_ref.shape[1]
    start = pl.multiple_of(meta[0] * rows, rows)

    def through(values, part):
        return dot(values[:, :half], weights_ref[0, part], NT) + dot(values[:, half:], weights_ref[1, part], NT)

    def from_keys(at):
        return through(dkl_ref[at, :], 1) + through(dvl_ref[at, :], 2)

    slope_own_ref[...] += through(joined(dq_ref), 0) + from_keys(pl.ds(start, rows))
    slope_oth_ref[...] = from_keys(pl.ds(pl.multiple_of(rows - start, rows), rows)).astype(BF)


class Moves:
    def __init__(self, sems):
        self.sems, self.used = sems, 0

    def start(self, source, target):
        copy = pltpu.make_async_copy(source, target, self.sems.at[self.used])
        self.used += 1
        copy.start()
        return copy


def wait(*copies):
    for copy in copies:
        copy.wait()


def rows_at(index, rows):
    return pl.ds(pl.multiple_of(index * rows, rows), rows)


def gather_entries(moves, meta, i, target):
    rows = i.entry_own.shape[0]
    return [
        moves.start(i.entry_own, target.at[rows_at(meta[0], rows), :]),
        moves.start(i.entry_oth, target.at[rows_at(1 - meta[0], rows), :]),
    ]


def fetch_heads_weights(moves, i, s):
    return [moves.start(i.own, s.weights.at[0]), moves.start(i.oth, s.weights.at[1])]


def fetch_feed_weights(moves, i, s):
    return [
        moves.start(source, target.at[side])
        for target, pair in ((s.comb, (i.comb0, i.comb1)), (s.exp_w, (i.exp0, i.exp1)), (s.red, (i.red0, i.red1)))
        for side, source in enumerate(pair)
    ]


def fetch(moves, i, s, *names):
    return [moves.start(getattr(i, name), getattr(s, name)) for name in names]


def as_row(square):
    return jnp.concatenate([square[r : r + 1, :] for r in range(square.shape[0])], axis=1)


def prepare(i, o, s):
    n_cells = i.lengths.shape[1]
    known = (i.known[...] > 0).astype(F32)
    chosen = (i.chosen[...] > 0).astype(F32)
    seen = jnp.maximum(known, chosen)
    block = known.shape[0]
    both = jnp.concatenate([known, seen], axis=0).astype(BF)
    row = lax.broadcasted_iota(jnp.int32, (PAIR, PAIR), 0)
    lane = lax.broadcasted_iota(jnp.int32, (PAIR, PAIR), 1)
    within = dot(both, (row < lane).astype(BF))
    totals = dot(both, jnp.ones((PAIR, PAIR), BF)).astype(BF)
    row = lax.broadcasted_iota(jnp.int32, (2 * block, 2 * block), 0)
    lane = lax.broadcasted_iota(jnp.int32, (2 * block, 2 * block), 1)
    earlier = ((lane < row) & ((lane < block) == (row < block))).astype(BF)
    places = jnp.where(both.astype(F32) > 0.5, within + dot(earlier, totals), -1.0)
    s.ranks[...] = jnp.concatenate(
        [as_row(places[:block]), as_row(places[block:]), jnp.zeros((6, s.ranks.shape[1]), F32)], axis=0
    )
    s.flags[...] = jnp.concatenate(
        [as_row(known), as_row(seen), as_row(chosen), jnp.zeros((13, s.flags.shape[1]), F32)], axis=0
    ).astype(BF)
    position = lax.broadcasted_iota(jnp.int32, known.shape, 0) * PAIR + lax.broadcasted_iota(jnp.int32, known.shape, 1)
    o.meta[0] = lax.axis_index("tensor").astype(jnp.int32)
    end = 0
    for c in range(n_cells):
        end = end + i.lengths[0, c]
        o.meta[1 + c] = end
        for turn, shown in enumerate((known, seen)):
            count = jnp.sum(jnp.where(position < end, shown, 0.0))
            o.meta[1 + n_cells * (1 + turn) + c] = count.astype(jnp.int32)
    s.vec[...] = jnp.concatenate(
        [
            *(ref[...].reshape(1, -1) for ref in (i.baseline, i.scales, i.shifts, i.adjustment, i.rescales, i.reshifts)),
            jnp.concatenate([i.thr0[...].astype(F32).reshape(1, -1), i.thr1[...].astype(F32).reshape(1, -1)], axis=1),
            jnp.concatenate([i.off0[...], i.off1[...]], axis=1),
            jnp.zeros((7, s.vec.shape[1]), F32),
        ],
        axis=0,
    )


def first_kernel(i, o, s):
    moves, meta = Moves(s.sems), o.meta
    rows = i.entry_own.shape[0]
    weights = fetch_heads_weights(moves, i, s)
    prepare(i, o, s)
    early = gather_entries(moves, meta, i, s.entry_all) + weights
    late = fetch_feed_weights(moves, i, s)
    saved = fetch(moves, s, o, "flags", "ranks", "vec")
    key_marks(meta, 0, s.marks)
    select_keys(meta, 0, s.ranks, s.sel)
    wait(*early)
    entry_own = s.entry_all[rows_at(meta[0], rows), :]
    project(meta, 0, entry_own, s.entry_all, s.weights, s.vec, s.sel, s.q, s.k, s.v, s.ko, s.vo)
    saved += fetch(moves, s, o, "q", "k", "v", "ko", "vo")
    attend(meta, 0, s.flags, s.q, s.k, s.v, s.ko, s.vo, s.marks, s.closed, s.off, s.top, s.edge, s.ctx, s.lse)
    saved += fetch(moves, s, o, "ctx", "lse")
    wait(*late)
    entry_own = s.entry_all[rows_at(meta[0], rows), :]
    result = feed_forward(entry_own, s.ctx, s.comb, s.exp_w, s.red, s.vec, s.before, s.unit1, s.unit2, s.rs)
    low = result.astype(BF)
    chosen = flag_column(meta, s.flags, 2, rows)[:, :1] > 0.5
    s.second[...] = jnp.where(chosen, low, entry_own)
    s.low[...] = low
    saved += fetch(moves, s, o, "second", "low", "before", "unit1", "unit2", "rs")
    wait(*saved)


def second_kernel(i, o, s):
    moves, meta = Moves(s.sems), i.meta
    rows = i.entry_own.shape[0]
    first = fetch(moves, i, s, "ranks", "flags", "vec")
    early = gather_entries(moves, meta, i, s.entry_all) + fetch_heads_weights(moves, i, s)
    late = fetch_feed_weights(moves, i, s) + fetch(moves, i, s, "cotangent")
    key_marks(meta, 1, s.marks)
    wait(*first)
    select_keys(meta, 1, s.ranks, s.sel)
    wait(*early)
    saved = fetch(moves, s, o, "entry_all")
    entry_own = s.entry_all[rows_at(meta[0], rows), :]
    project(meta, 1, entry_own, s.entry_all, s.weights, s.vec, s.sel, s.q, s.k, s.v, s.ko, s.vo)
    attend(meta, 1, s.flags, s.q, s.k, s.v, s.ko, s.vo, s.marks, s.closed, s.off, s.top, s.edge, s.ctx, s.lse)
    saved += fetch(moves, s, o, "ctx")
    wait(*late)
    entry_own = s.entry_all[rows_at(meta[0], rows), :]
    result = feed_forward(entry_own, s.ctx, s.comb, s.exp_w, s.red, s.vec, s.before, s.unit1, s.unit2, s.rs)
    s.low[...] = result.astype(BF)
    saved += fetch(moves, s, o, "low")
    mixture_slope, sums = feed_backward(s.cotangent[...].astype(F32), s.before, s.unit1, s.unit2, s.rs, s.comb, s.exp_w, s.red, s.vec, s.hid, s.sl, s.nl, s.bl, s.ml, s.do)
    s.sums[...] = padded(sums, s.sums)
    s.slope_own[...] = mixture_slope
    saved += fetch(moves, s, o, "hid", "sl", "nl", "bl", "ml", "sums")
    attend_backward(meta, 1, s.flags, s.q, s.k, s.v, s.ko, s.vo, s.marks, s.closed, s.ctx, s.lse, s.do, s.sel,
                    s.dq, s.dk, s.dv, s.dko, s.dvo, s.dkl, s.dvl)
    saved += fetch(moves, s, o, "dq", "dkl", "dvl")
    entry_slopes(meta, s.weights, s.dq, s.dkl, s.dvl, s.slope_own, s.slope_oth)
    saved += fetch(moves, s, o, "slope_oth", "slope_own")
    wait(*saved)


def padded(sums, like):
    return jnp.concatenate(sums + [jnp.zeros((like.shape[0] - len(sums), like.shape[1]), F32)], axis=0)


def side_by_side(matrix, rows):
    return jnp.concatenate([matrix[:rows], matrix[rows:]], axis=1)


def head_weights(meta, entry_all, dq_ref, dk, dv):
    rows = dq_ref.shape[1]
    dq = joined(dq_ref)
    parts = (dot(entry_all[rows_at(meta[0], rows), :], dq, TN), dot(entry_all[...], dk, TN), dot(entry_all[...], dv, TN))
    return parts, jnp.sum(dq.astype(F32), axis=0, keepdims=True), jnp.sum(dv.astype(F32), axis=0, keepdims=True)


def feed_weights(hid_ref, sl_ref, nl_ref, bl_ref, ctx_ref, ml_ref):
    return (
        dot(joined(ctx_ref), ml_ref[...], TN),
        dot(nl_ref[...], bl_ref[...], TN),
        dot(hid_ref[...], sl_ref[...], TN),
    )


def back_kernel(i, o, s):
    moves, meta = Moves(s.sems), i.meta
    first = fetch(moves, i, s, "flags", "cotangent", "slope_recv", "slope_own", "unit2", "rs")
    early = fetch(moves, i, s, "unit1", "vec", "before") + fetch_feed_weights(moves, i, s)
    next_ = fetch(moves, i, s, "ranks", "q", "ctx", "lse", "ko", "vo", "k", "v")
    late = fetch(moves, i, s, "sums2", "ctx2", "ml2", "nl2", "bl2", "hid2", "sl2")
    last = gather_entries(moves, meta, i, s.entry_all) + fetch_heads_weights(moves, i, s)
    last += fetch(moves, i, s, "entry2", "dq2", "dkl2", "dvl2")
    rows = i.slope_own.shape[0]
    half = i.comb0.shape[1] // 2
    key_marks(meta, 0, s.marks)
    wait(*first)
    chosen = flag_column(meta, s.flags, 2, rows)[:, :1] > 0.5
    second_slope = s.slope_own[...] + s.slope_recv[...].astype(F32)
    incoming = s.cotangent[...].astype(F32) + jnp.where(chosen, second_slope, 0.0)
    s.slope[...] = jnp.where(chosen, 0.0, second_slope)
    wait(*early)
    mixture_slope, sums = feed_backward(incoming, s.before, s.unit1, s.unit2, s.rs, s.comb, s.exp_w, s.red, s.vec, s.hid, s.sl, s.nl, s.bl, s.ml, s.do)
    s.slope[...] += mixture_slope
    s.sums[...] = padded(sums, s.sums)
    wait(*next_)
    select_keys(meta, 0, s.ranks, s.sel)
    attend_backward(meta, 0, s.flags, s.q, s.k, s.v, s.ko, s.vo, s.marks, s.closed, s.ctx, s.lse, s.do, s.sel,
                    s.dq, s.dk, s.dv, s.dko, s.dvo, s.dkl, s.dvl)
    wait(*late)
    for part, (left, right) in enumerate(zip(
        feed_weights(s.hid, s.sl, s.nl, s.bl, s.ctx, s.ml), feed_weights(s.hid2, s.sl2, s.nl2, s.bl2, s.ctx2, s.ml2)
    )):
        total = left + right
        for side, out in ((1, s.feed_oth), (0, s.feed_own)):
            mine = slice(side * half, (side + 1) * half)
            block = side_by_side(total[:, mine], half) if part == 1 else total[mine]
            out[part * half : (part + 1) * half] = block.astype(BF)
    saved = fetch(moves, s, o, "feed_oth", "feed_own")
    wait(*last)
    parts, q_sum, v_sum = head_weights(meta, s.entry_all, s.dq, s.dkl[...], s.dvl[...])
    parts2, q_sum2, v_sum2 = head_weights(meta, s.entry2, s.dq2, s.dkl2[...], s.dvl2[...])
    for c in range(3):
        total = parts[c] + parts2[c]
        for side, out in ((1, s.heads_oth), (0, s.heads_own)):
            cols = slice(side * half, (side + 1) * half)
            out[c * half : (c + 1) * half] = side_by_side(total[:, cols], half).astype(BF)
    s.sums[...] += s.sums2[...]
    s.sums[7:8, :] = q_sum + q_sum2
    s.sums[8:9, :] = v_sum + v_sum2
    saved += fetch(moves, s, o, "heads_oth", "heads_own", "sums")
    entry_slopes(meta, s.weights, s.dq, s.dkl, s.dvl, s.slope, s.slope_oth)
    saved += fetch(moves, s, o, "slope_oth", "slope")
    wait(*saved)


def call(kernel, micros, ins, outs, scratch):
    spaces = {"s": pltpu.SMEM, "v": pltpu.VMEM, "h": pl.ANY}
    scratch = scratch | {name: like for name, like in outs.items() if name != "meta"}
    in_names, out_names, scratch_names = list(ins), list(outs), list(scratch)

    def body(*refs):
        a, b = len(in_names), len(in_names) + len(out_names)
        kernel(
            types.SimpleNamespace(**dict(zip(in_names, refs[:a]))),
            types.SimpleNamespace(**dict(zip(out_names, refs[a:b]))),
            types.SimpleNamespace(sems=refs[-1], **dict(zip(scratch_names, refs[b:-1]))),
        )

    results = pl.pallas_call(
        body,
        out_shape=[jax.ShapeDtypeStruct(shape, kind) for shape, kind in outs.values()],
        in_specs=[pl.BlockSpec(memory_space=spaces[place]) for _, place in ins.values()],
        out_specs=[pl.BlockSpec(memory_space=pltpu.SMEM if name == "meta" else pl.ANY) for name in outs],
        scratch_shapes=[pltpu.VMEM(shape, kind) for shape, kind in scratch.values()] + [pltpu.SemaphoreType.DMA((48,))],
        compiler_params=pltpu.CompilerParams(vmem_limit_bytes=LIMITS[kernel.__name__] * 2**20),
        cost_estimate=pl.CostEstimate(flops=int(micros * 1.1e9), bytes_accessed=0, transcendentals=0),
    )(*[array for array, _ in ins.values()])
    return dict(zip(out_names, results))


def partner(value):
    return lax.ppermute(value, "tensor", [(0, 1), (1, 0)])


def flip(value, size, step):
    return lax.ppermute(value, "dp", [(i, i ^ step) for i in range(size)])


def tree_sum(parts):
    parts = list(parts)
    while len(parts) > 1:
        parts = [parts[i] + parts[i + 1] for i in range(0, len(parts), 2)]
    return parts[0]


def digits(size):
    out, stride = [], 1
    while stride < size:
        radix = 4 if size % (stride * 4) == 0 else 2
        out.append((stride, radix))
        stride *= radix
    return out


def sum_small(value, size):
    for stride, radix in digits(size):
        parts = [value] + [flip(value, size, k * stride) for k in range(1, radix)]
        value = tree_sum(parts)
    return value


def sum_large(value, size):
    me = lax.axis_index("dp")
    rows, width = value.shape
    order = jnp.arange(size, dtype=jnp.int32) ^ me
    value = jnp.take(value.reshape(size, rows // size, width), order, axis=0)
    shape = [radix for _, radix in digits(size)]
    value = value.reshape(shape[::-1] + [rows // size, width])
    n = len(shape)
    steps = range(n)
    for step in steps:
        stride, radix = digits(size)[step]
        axis = n - 1 - step
        take = lambda k: lax.index_in_dim(value, k, axis, keepdims=True)
        parts = [take(0).astype(F32)] + [flip(take(k), size, k * stride).astype(F32) for k in range(1, radix)]
        value = tree_sum(parts).astype(BF)
    for step in reversed(steps):
        stride, radix = digits(size)[step]
        axis = n - 1 - step
        value = jnp.concatenate([value] + [flip(value, size, k * stride) for k in range(1, radix)], axis=axis)
    value = value.reshape(size, rows // size, width)
    return jnp.take(value, order, axis=0).reshape(rows, width)


QUAD = 4


def target_of(place, first, second):
    return place[0] ^ jnp.where(place[1] == 0, second * QUAD + first, first * QUAD + second)


def spread_kernel(place, ins, out):
    feed_own, feed_recv, heads_own, heads_recv, vec_own, vec_recv = ins
    chunk = feed_own.shape[0] // QUAD**2
    half = vec_own.shape[1] // 2
    own, recv = vec_own[...], vec_recv[...]
    own_side = own[6:9, :half] + recv[6:9, half:]
    vec = jnp.concatenate(
        [own[:6] + recv[:6], jnp.concatenate([own_side, jnp.zeros_like(own_side)], axis=1), jnp.zeros_like(own[9:])], axis=0
    ).astype(BF)
    for first in range(QUAD):
        out[first][2 * QUAD * chunk :, :] = vec
        for second in range(QUAD):
            target = target_of(place, first, second)
            at = pl.ds(pl.multiple_of(target * chunk, 16), chunk)
            for n, (left, right) in enumerate(((feed_own, feed_recv), (heads_own, heads_recv))):
                total = left[at, :].astype(F32) + right[at, :].astype(F32)
                start = (2 * second + n) * chunk
                out[first][start : start + chunk, :] = total.astype(BF)


def added(refs, at):
    parts = [ref[at, :].astype(F32) for ref in refs]
    return (parts[0] + parts[1]) + (parts[2] + parts[3])


def between_kernel(got, out):
    tall = (got[0].shape[0] - 16) // QUAD
    vec = added(got, slice(QUAD * tall, QUAD * tall + 16)).astype(BF)
    for k in range(QUAD):
        out[k][:tall, :] = added(got, slice(k * tall, (k + 1) * tall)).astype(BF)
        out[k][tall:, :] = vec


def ended_kernel(got, out):
    tall = got[0].shape[0] - 16
    out[0][...] = added(got, slice(0, tall)).astype(BF)
    out[1][...] = added(got, slice(tall, tall + 16))


def stack_kernel(got, out):
    for k in range(QUAD):
        out[0][k] = got[k][...]


def unfold(matrix):
    half = matrix.shape[1] // 2
    return jnp.concatenate([matrix[:, :half], matrix[:, half:]], axis=0)


def collect_kernel(place, got, out, s):
    chunk = s.feed.shape[0] // QUAD**2
    rows = s.feed.shape[0] // 3
    for first in range(QUAD):
        for second in range(QUAD):
            target = target_of(place, first, second)
            at = pl.ds(pl.multiple_of(target * chunk, 16), chunk)
            for n, into in enumerate((s.feed, s.heads)):
                into[at, :] = got[first][second, chunk * n : chunk * (n + 1), :].astype(F32)
    for c in range(3):
        out.heads[c] = unfold(s.heads[c * rows : (c + 1) * rows, :])
    out.comb[...] = s.feed[:rows, :]
    out.exp_w[...] = unfold(s.feed[rows : 2 * rows, :])
    out.red[...] = s.feed[2 * rows :, :]


def plain_call(body, args, outs, scratch=()):
    return pl.pallas_call(
        body,
        out_shape=[jax.ShapeDtypeStruct(shape, kind) for shape, kind in outs],
        in_specs=[pl.BlockSpec(memory_space=pltpu.SMEM if a.dtype == jnp.int32 else pltpu.VMEM) for a in args],
        out_specs=[pl.BlockSpec(memory_space=pltpu.VMEM)] * len(outs),
        scratch_shapes=list(scratch),
        compiler_params=pltpu.CompilerParams(vmem_limit_bytes=LIMITS["small"] * 2**20),
    )(*args)


def sum_quads(size, feed, heads, vec, beside):
    rows, width = feed[0].shape
    half = width // 2
    side = lax.axis_index("tensor").astype(jnp.int32)
    place = jnp.stack([lax.axis_index("dp").astype(jnp.int32), side])
    tall = 2 * (rows // QUAD**2)

    def spread_body(*refs):
        spread_kernel(refs[0], refs[1:7], refs[7:])

    def four(kernel):
        return lambda *refs: kernel(refs[:QUAD], refs[QUAD:])

    def exchange(parts, steps):
        got = [parts[0]]
        for k in range(1, QUAD):
            perm = [(2 * n + core, 2 * (n ^ (k * steps[core])) + core) for n in range(size) for core in range(2)]
            got.append(lax.ppermute(parts[k], ("dp", "tensor"), perm))
        return got

    parts = plain_call(spread_body, [place, *feed, *heads, *vec], [((QUAD * tall + 16, width), BF)] * QUAD)
    parts = plain_call(four(between_kernel), exchange(parts, (1, QUAD)), [((tall + 16, width), BF)] * QUAD)
    total, vectors = plain_call(four(ended_kernel), exchange(parts, (QUAD, 1)), [((tall, width), BF), ((16, width), F32)])
    shared = jnp.where(side == 0, vectors, partner(vectors))
    total, beside = lax.optimization_barrier((total, beside))
    (total,) = plain_call(four(stack_kernel), exchange([total] * QUAD, (QUAD, 1)), [((QUAD, tall, width), BF)])
    got = exchange([total] * QUAD, (1, QUAD))

    def collect_body(*refs):
        outs = types.SimpleNamespace(**dict(zip(("heads", "comb", "exp_w", "red"), refs[5:9])))
        collect_kernel(refs[0], refs[1:5], outs, types.SimpleNamespace(feed=refs[9], heads=refs[10]))

    totals = plain_call(
        collect_body,
        [place, *got],
        [((3, width, half), F32), ((half, width), F32), ((width, half), F32), ((half, width), F32)],
        [pltpu.VMEM((rows, width), F32)] * 2,
    )
    return (*totals, vectors[7:9, :half], vectors[6:7, :half], *(shared[n] for n in range(6))), beside


def sum_any(size, feed, heads, vec, beside):
    half = feed[0].shape[1] // 2
    width = 2 * half
    total = lambda pair: sum_large((pair[0].astype(F32) + pair[1].astype(F32)).astype(BF), size).astype(F32)
    feed, heads = total(feed), total(heads).reshape(3, half, width)
    own, recv = vec
    sides = jnp.pad(own[6:9, :half] + recv[6:9, half:], ((0, 0), (0, half)))
    vec = sum_small(jnp.concatenate([own[:6] + recv[:6], sides], axis=0), size)
    return (
        jnp.stack([unfold(heads[c]) for c in range(3)]), feed[:half], unfold(feed[half : 2 * half]), feed[2 * half :],
        vec[7:9, :half], vec[6:7, :half], *(vec[c : c + 1] for c in range(6)),
    ), beside


def on_device(dp, tokens, first_cotangent, second_cotangent, projection, offsets, combiner, baseline, scales, shifts,
              expander, thresholds, reducer, adjustment, rescales, reshifts, known_flags, chosen_flags, cell_lengths):
    rows, width = tokens.shape
    group = known_flags.shape[0]
    half = projection.shape[2]
    pairs = 2 * half // PAIR
    n_cells = cell_lengths.shape[1]
    entry_oth, oth, comb1, exp1, red1, offsets_oth, thresholds_oth = (
        partner(v) for v in (tokens, projection, combiner, expander, reducer, offsets, thresholds)
    )
    small_in = {
        "lengths": (cell_lengths, "s"), "known": (known_flags.reshape(-1, PAIR), "v"), "chosen": (chosen_flags.reshape(-1, PAIR), "v"),
        "baseline": (baseline, "v"), "scales": (scales, "v"), "shifts": (shifts, "v"), "adjustment": (adjustment, "v"),
        "rescales": (rescales, "v"), "reshifts": (reshifts, "v"), "thr0": (thresholds, "v"), "thr1": (thresholds_oth, "v"), "off0": (offsets, "v"), "off1": (offsets_oth, "v"),
    }
    square, square32 = ((rows, width), BF), ((rows, width), F32)
    spread = ((rows, PAIR), F32)
    own_pairs, own_pairs32 = ((pairs, rows, PAIR), BF), ((pairs, rows, PAIR), F32)
    all_pairs, all_pairs32 = ((pairs, group, PAIR), BF), ((pairs, group, PAIR), F32)
    entries, grads_like, sums_like = ((group, width), BF), ((3 * half, width), BF), ((16, width), F32)
    square3 = ((3, width, width), F32)
    comb_like, exp_like = ((2,) + combiner.shape, BF), ((2,) + expander.shape, BF)
    weights_like = {"weights": ((2,) + projection.shape, BF), "comb": comb_like, "exp_w": exp_like, "red": comb_like}
    state_like = {
        "entry_all": entries, "sel": ((group, group), BF), "marks": ((group, PAIR), BF), "q": own_pairs, "k": all_pairs, "v": all_pairs,
        "ko": own_pairs, "vo": own_pairs, "ctx": own_pairs, "lse": own_pairs32, "before": square32, "unit1": square32, "unit2": square32, "rs": spread,
    }
    made_like = {"hid": square, "sl": square, "nl": square, "bl": square, "ml": square}
    back_scratch = {"closed": spread, "dk": all_pairs32, "dv": all_pairs32, "dko": own_pairs32, "dvo": own_pairs32}
    slopes_like = {"dq": own_pairs, "dkl": entries, "dvl": entries}
    saved_names = tuple(name for name in state_like if name not in ("entry_all", "sel", "marks"))
    heads_names = ("q", "k", "v", "ko", "vo", "lse", "ctx")
    norm_names = ("before", "unit1", "unit2", "rs")
    closed = {
        "closed": spread, "off": own_pairs32, "top": ((pairs, rows // Q_TILE, 2 * Q_TILE, PAIR), F32), "edge": ((2, 8, PAIR), F32),
    }
    likes = lambda names: {name: state_like[name] for name in names}
    feed_like = {name: weights_like[name] for name in ("comb", "exp_w", "red")}
    small_like = {"flags": ((16, group), BF), "ranks": ((8, group), F32), "vec": sums_like}
    heads_in = {"own": (projection, "h"), "oth": (oth, "h")}
    feed_in = {name: (array, "h") for name, array in (
        ("comb0", combiner), ("comb1", comb1), ("exp0", expander), ("exp1", exp1), ("red0", reducer), ("red1", red1))}
    held = lambda values, *names: {name: (values[name], "h") for name in names}

    one = call(
        first_kernel, 13,
        small_in | {"entry_own": (tokens, "h"), "entry_oth": (entry_oth, "h")} | heads_in | feed_in,
        {"meta": ((1 + 3 * n_cells,), jnp.int32), "low": square, "second": square} | small_like | likes(saved_names),
        closed | weights_like | likes(("entry_all", "sel", "marks")),
    )
    second_oth = partner(one["second"])
    table = {"meta": (one["meta"], "s")} | held(one, *small_like)
    two = call(
        second_kernel, 28,
        table | {"entry_own": (one["second"], "h"), "entry_oth": (second_oth, "h"), "cotangent": (second_cotangent, "h")} | heads_in | feed_in,
        {"low": square, "slope_oth": square, "slope_own": square32, "sums": sums_like} | likes(("entry_all", "ctx")) | made_like | slopes_like,
        closed | small_like | weights_like | state_like | back_scratch | {"cotangent": square, "do": own_pairs},
    )
    slope_recv = partner(two["slope_oth"])
    kept_names = tuple(made_like) + ("ctx", "sums") + tuple(slopes_like)
    kept_like = {name + "2": (made_like | slopes_like | {"ctx": own_pairs, "sums": sums_like})[name] for name in kept_names}
    last = call(
        back_kernel, 25,
        table | heads_in | feed_in
        | {"entry_own": (tokens, "h"), "entry_oth": (entry_oth, "h"), "cotangent": (first_cotangent, "h"), "slope_recv": (slope_recv, "h")}
        | held(one, *heads_names, *norm_names) | held(two, "slope_own")
        | {name + "2": (two[name], "h") for name in kept_names} | {"entry2": (two["entry_all"], "h")},
        {"slope": square32, "slope_oth": square, "sums": sums_like, "feed_own": grads_like, "feed_oth": grads_like, "heads_own": grads_like, "heads_oth": grads_like},
        small_like | weights_like | made_like | kept_like | slopes_like | state_like | back_scratch
        | {"entry2": entries, "cotangent": square, "slope_recv": square, "slope_own": square32, "do": own_pairs},
    )
    tokens_gradient = last["slope"] + partner(last["slope_oth"]).astype(F32)
    summed, tokens_gradient = (sum_quads if dp == QUAD**2 else sum_any)(
        dp,
        (last["feed_own"], partner(last["feed_oth"])),
        (last["heads_own"], partner(last["heads_oth"])),
        (last["sums"], partner(last["sums"])),
        tokens_gradient,
    )
    heads_total, comb_total, exp_total, red_total, off_total, thr_total, *vectors = summed
    base_total, scale_total, shift_total, adjust_total, rescale_total, reshift_total = (v.reshape(-1) for v in vectors)
    return (
        one["low"],
        two["low"],
        tokens_gradient,
        heads_total,
        off_total,
        comb_total,
        base_total,
        scale_total,
        shift_total,
        exp_total,
        thr_total.reshape(-1),
        red_total,
        adjust_total,
        rescale_total,
        reshift_total,
    )


def solution(mesh):
    rows = P(("dp", "tensor"), None)
    return jax.shard_map(
        functools.partial(on_device, mesh.shape["dp"]),
        mesh=mesh,
        in_specs=(
            rows, rows, rows, P(None, None, "tensor"), P(None, "tensor"), P("tensor", None), P(), P(), P(),
            P(None, "tensor"), P("tensor"), P("tensor", None), P(), P(), P(), P("dp"), P("dp"), P("dp", None),
        ),
        out_specs=(
            rows, rows, rows, P(None, None, "tensor"), P(None, "tensor"), P("tensor", None), P(), P(), P(),
            P(None, "tensor"), P("tensor"), P("tensor", None), P(), P(), P(),
        ),
        check_vma=False,
    )
```

```python
import functools
import types

import jax
import jax.numpy as jnp
from jax import lax
from jax.experimental import pallas as pl
from jax.experimental.pallas import tpu as pltpu
from jax.sharding import PartitionSpec as P

HD = 64
PAIR = 2 * HD
BF = jnp.bfloat16
F32 = jnp.float32
HIDE = -1e30
SAFE = 60.0
LEAST = 1e-26
NN = (((1,), (0,)), ((), ()))
NT = (((1,), (1,)), ((), ()))
TN = (((0,), (0,)), ((), ()))
LIMITS = {"first_kernel": 58, "second_kernel": 58, "back_kernel": 58, "slopes_kernel": 58, "small": 24}
UNROLL_FORWARD = 2
UNROLL_BACKWARD = 1
Q_TILE = 256
K_TILE = 256
WINDOWS = (128, 256, 384, 512, 640)


def dot(left, right, dims=NN):
    return lax.dot_general(left, right, dims, preferred_element_type=F32)


def lanes_of(rows):
    return lax.broadcasted_iota(jnp.int32, (rows, PAIR), 1)


def cells_of(meta):
    return (meta.shape[0] - 1) // 3


def row_cells(start, rows, meta, bounds):
    position = start + lax.broadcasted_iota(jnp.int32, (rows, PAIR), 0)
    cell = jnp.zeros((rows, PAIR), jnp.int32)
    for c in bounds:
        cell = cell + (position >= meta[c]).astype(jnp.int32)
    return cell


def norm_forward(values, gain, shift):
    centered = values - jnp.mean(values, axis=-1, keepdims=True)
    inverse = lax.rsqrt(jnp.mean(centered * centered, axis=-1, keepdims=True) + 1e-05)
    unit = centered * inverse
    return unit * gain + shift, unit, inverse


def norm_backward(gradient, unit, inverse, gain):
    scaled = gradient * gain
    projected = (
        scaled
        - jnp.mean(scaled, axis=-1, keepdims=True)
        - unit * jnp.mean(scaled * unit, axis=-1, keepdims=True)
    )
    return (
        projected * inverse,
        jnp.sum(gradient * unit, axis=0, keepdims=True),
        jnp.sum(gradient, axis=0, keepdims=True),
    )


def key_marks(meta, turn, marks_ref):
    rows = marks_ref.shape[0]
    n_cells = cells_of(meta)
    lane = lanes_of(rows)
    first = 1 + n_cells * (1 + turn)
    cell = row_cells(0, rows, meta, range(first, first + n_cells))
    marks_ref[...] = jnp.where(
        lane < n_cells,
        jnp.where(cell == lane, 0.0, HIDE),
        jnp.where((lane % HD >= n_cells) & (lane % HD < n_cells + 3), -1.0, 0.0),
    ).astype(BF)


def flag_column(meta, flags, row, rows):
    pick = (lax.broadcasted_iota(jnp.int32, (flags.shape[0], PAIR), 0) == row).astype(BF)
    start = pl.multiple_of(meta[0] * rows, rows)
    return dot(flags[:, pl.ds(start, rows)], pick, TN)


def key_tiles(meta, turn):
    count = meta[n_bounds(meta, turn)]
    return jnp.maximum((count + K_TILE - 1) // K_TILE, 1)


def n_bounds(meta, turn):
    return cells_of(meta) * (2 + turn)


def select_keys(meta, turn, ranks, sel_ref):
    keys_all = ranks.shape[1]
    tiles = key_tiles(meta, turn)
    place = ranks[turn : turn + 1, :]
    for tile in range(keys_all // K_TILE):

        @pl.when(tile < tiles)
        def _():
            row = (lax.broadcasted_iota(jnp.int32, (K_TILE, keys_all), 0) + tile * K_TILE).astype(F32)
            sel_ref[tile * K_TILE : (tile + 1) * K_TILE, :] = (row == place).astype(BF)


def spread_pairs(ref, side, half, at, values):
    for part in range(half // PAIR):
        ref[side * (half // PAIR) + part, at, :] = values[:, part * PAIR : (part + 1) * PAIR]


def project(meta, turn, entry_own, entry_all, weights_ref, vec, sel_ref, q_ref, k_ref, v_ref, ko_ref, vo_ref):
    half = weights_ref.shape[3]
    every = slice(None)
    for side in range(2):
        cols = slice(side * half, (side + 1) * half)
        queries = (dot(entry_own, weights_ref[side, 0]) + vec[7:8, cols]).astype(BF) * 0.125
        spread_pairs(q_ref, side, half, every, queries.astype(BF))
        spread_pairs(ko_ref, side, half, every, dot(entry_own, weights_ref[side, 1]).astype(BF))
        spread_pairs(vo_ref, side, half, every, (dot(entry_own, weights_ref[side, 2]) + vec[8:9, cols]).astype(BF))
    tiles = key_tiles(meta, turn)
    for tile in range(entry_all.shape[0] // K_TILE):
        at = slice(tile * K_TILE, (tile + 1) * K_TILE)

        @pl.when(tile < tiles)
        def _():
            entry = dot(sel_ref[at, :], entry_all[...]).astype(BF)
            for side in range(2):
                cols = slice(side * half, (side + 1) * half)
                spread_pairs(k_ref, side, half, at, dot(entry, weights_ref[side, 1]).astype(BF))
                spread_pairs(v_ref, side, half, at, (dot(entry, weights_ref[side, 2]) + vec[8:9, cols]).astype(BF))

        @pl.when(tile >= tiles)
        def _():
            k_ref[:, at, :] = jnp.zeros((k_ref.shape[0], K_TILE, PAIR), BF)
            v_ref[:, at, :] = jnp.zeros((v_ref.shape[0], K_TILE, PAIR), BF)


def for_windows(meta, turn, rows, keys_all, body):
    n_cells = cells_of(meta)
    ends, seen = 1, 1 + n_cells * (1 + turn)

    def one_tile(tile, carried):
        first = meta[0] * rows + tile * Q_TILE
        last = first + Q_TILE - 1
        low, high = 0, meta[seen + n_cells - 1]
        for c in range(n_cells - 1):
            low = jnp.where(first >= meta[ends + c], meta[seen + c], low)
            d = n_cells - 2 - c
            high = jnp.where(last < meta[ends + d], meta[seen + d], high)
        low = (low // 16) * 16
        need = high - low
        below = -1
        for width in WINDOWS + (keys_all,):
            start = pl.multiple_of(jnp.minimum(low, keys_all - width), 16)

            @pl.when((need > below) & (need <= width))
            def _():
                body(tile, start, width)

            below = width
        return carried

    lax.fori_loop(0, rows // Q_TILE, one_tile, 0)


def head_sums(values):
    high = values.astype(BF)
    low = (values - high.astype(F32)).astype(BF)
    row = lax.broadcasted_iota(jnp.int32, (2 * PAIR, PAIR), 0) % PAIR
    lane = lax.broadcasted_iota(jnp.int32, (2 * PAIR, PAIR), 1)
    ones = ((row < HD) == (lane < HD)).astype(BF)
    return dot(jnp.concatenate([high, low], axis=1), ones)


def by_head(values):
    lane = lax.broadcasted_iota(jnp.int32, values.shape, 1)
    zero = jnp.zeros_like(values)
    return jnp.concatenate([jnp.where(lane < HD, values, zero), jnp.where(lane < HD, zero, values)], axis=0)


def merge_heads(values):
    rows = values.shape[0] // 2
    lane = lanes_of(rows)
    return jnp.where(lane < HD, values[:rows], values[rows:])


def own_places(meta, first, rows):
    n_cells = cells_of(meta)
    lane = lanes_of(rows)
    cell = row_cells(first, rows, meta, range(1, n_cells))
    return jnp.where((cell == lane) & (lane < n_cells), 1.0, 0.0)


def row_tails(place, offset, n_cells):
    lane = lanes_of(offset.shape[0])
    side = lane % HD
    high = offset.astype(BF).astype(F32)
    middle = (offset - high).astype(BF).astype(F32)
    taken = jnp.where(
        side == n_cells,
        high,
        jnp.where(side == n_cells + 1, middle, jnp.where(side == n_cells + 2, offset - high - middle, 0.0)),
    )
    return jnp.concatenate(
        [jnp.where(lane < HD, taken, 0.0) + place, jnp.where(lane < HD, 0.0, taken) + place], axis=0
    ).astype(BF)


def attend(meta, turn, flags, q_ref, k_ref, v_ref, ko_ref, vo_ref, marks_ref, closed_ref, off_ref, top_ref, edge_ref, ctx_ref, lse_ref):
    pairs, rows = q_ref.shape[0], q_ref.shape[1]
    n_cells = cells_of(meta)
    lane = lanes_of(Q_TILE)
    closed_ref[...] = jnp.where(flag_column(meta, flags, turn, rows) > 0.5, HIDE, 0.0)
    off_ref[...] = jnp.zeros_like(off_ref)

    def own_scores(pair, at):
        product = q_ref[pair, at, :].astype(F32) * ko_ref[pair, at, :].astype(F32)
        return head_sums(product) + closed_ref[at, :] - off_ref[pair, at, :]

    def one_tile(tile, start, width):
        at = pl.ds(pl.multiple_of(tile * Q_TILE, Q_TILE), Q_TILE)
        place = own_places(meta, meta[0] * rows + tile * Q_TILE, Q_TILE)
        window = pl.ds(start, width)

        def one_pair(pair, carried):
            offset = off_ref[pair, at, :]
            keys = jnp.concatenate([k_ref[pair, window, :], marks_ref[window, :]], axis=1)
            vals = jnp.concatenate([v_ref[pair, window, :], jnp.ones((width, PAIR), BF)], axis=1)
            asked = jnp.concatenate([by_head(q_ref[pair, at, :]), row_tails(place, offset, n_cells)], axis=1)
            scores = dot(asked, keys, NT)
            mixed = dot(jnp.exp(scores).astype(BF), vals)
            top = scores[:, :PAIR]
            for part in range(1, width // PAIR):
                top = jnp.maximum(top, scores[:, part * PAIR : (part + 1) * PAIR])
            top_ref[pair, tile] = top
            self_score = own_scores(pair, at)
            self_weight = jnp.exp(self_score)
            total = merge_heads(mixed[:, PAIR:]) + self_weight
            context = (merge_heads(mixed[:, :PAIR]) + self_weight * vo_ref[pair, at, :].astype(F32)) / total
            ctx_ref[pair, at, :] = context.astype(BF)
            lse_ref[pair, at, :] = offset + jnp.log(total)
            highest = jnp.maximum(jnp.maximum(top[:Q_TILE], top[Q_TILE:]), self_score)
            edge_ref[0] = jnp.maximum(edge_ref[0], jnp.max(highest.reshape(-1, 8, PAIR), axis=0))
            edge_ref[1] = jnp.minimum(edge_ref[1], jnp.min(total.reshape(-1, 8, PAIR), axis=0))
            return carried

        lax.fori_loop(0, pairs, one_pair, 0, unroll=UNROLL_FORWARD)

    def attempt(_):
        edge_ref[0] = jnp.full(edge_ref.shape[1:], HIDE, F32)
        edge_ref[1] = jnp.ones(edge_ref.shape[1:], F32)
        for_windows(meta, turn, rows, k_ref.shape[1], one_tile)
        again = (jnp.max(edge_ref[0]) > SAFE) | (jnp.min(edge_ref[1]) < LEAST)

        @pl.when(again)
        def _():
            def raise_pair(index, carried):
                tile, pair = index // pairs, index % pairs
                at = pl.ds(pl.multiple_of(tile * Q_TILE, Q_TILE), Q_TILE)
                top = jnp.max(top_ref[pair, tile], axis=1, keepdims=True)
                tops = jnp.where(lane < HD, top[:Q_TILE], top[Q_TILE:])
                off_ref[pair, at, :] = off_ref[pair, at, :] + jnp.maximum(tops, own_scores(pair, at))
                return carried

            lax.fori_loop(0, pairs * (rows // Q_TILE), raise_pair, 0)

        return again.astype(jnp.int32)

    lax.while_loop(lambda again: again > 0, attempt, jnp.int32(1))


def joined(ref):
    return jnp.concatenate([ref[i] for i in range(ref.shape[0])], axis=1)


def feed_forward(entry_own, ctx_ref, comb, exp_w, red, vec, before_ref, unit1_ref, unit2_ref, rs_ref):
    context = joined(ctx_ref)
    half = comb.shape[1]
    attended = dot(context[:, :half], comb[0]) + dot(context[:, half:], comb[1])
    mixture = entry_own.astype(F32) + attended + vec[0:1, :]
    normed, unit1, inverse1 = norm_forward(mixture, vec[1:2, :], vec[2:3, :])
    unit1_ref[...] = unit1
    normed_low = normed.astype(BF)
    summed = normed + vec[3:4, :]
    for side in range(2):
        cols = slice(side * half, (side + 1) * half)
        before = dot(normed_low, exp_w[side]) + vec[6:7, cols]
        before_ref[:, cols] = before
        hidden = (0.5 * before * (1.0 + lax.erf(before * 0.7071067811865476))).astype(BF)
        summed = summed + dot(hidden, red[side])
    result, unit2, inverse2 = norm_forward(summed, vec[4:5, :], vec[5:6, :])
    unit2_ref[...] = unit2
    rows = result.shape[0]
    rs_ref[...] = jnp.where(lanes_of(rows) < HD, inverse1, inverse2)
    return result


def feed_backward(incoming, before_ref, unit1_ref, unit2_ref, rs_ref, comb, exp_w, red, vec, hid_ref, sl_ref, nl_ref, bl_ref, ml_ref, do_ref):
    half = comb.shape[1]
    inverse1 = rs_ref[:, :1]
    inverse2 = rs_ref[:, PAIR - 1 :]
    summed_slope, rescale_part, reshift_part = norm_backward(
        incoming, unit2_ref[...], inverse2, vec[4:5, :]
    )
    summed_low = summed_slope.astype(BF)
    sl_ref[...] = summed_low
    unit1 = unit1_ref[...]
    nl_ref[...] = (unit1 * vec[1:2, :] + vec[2:3, :]).astype(BF)
    normed_slope = summed_slope
    threshold_parts = []
    for side in range(2):
        cols = slice(side * half, (side + 1) * half)
        before = before_ref[:, cols]
        phi = 0.5 * (1.0 + lax.erf(before * 0.7071067811865476))
        hid_ref[:, cols] = (before * phi).astype(BF)
        slope = phi + before * jnp.exp(-0.5 * before * before) * 0.3989422804014327
        before_low = (dot(summed_low, red[side], NT) * slope).astype(BF)
        bl_ref[:, cols] = before_low
        threshold_parts.append(jnp.sum(before_low.astype(F32), axis=0, keepdims=True))
        normed_slope = normed_slope + dot(before_low, exp_w[side], NT)
    mixture_slope, scales_part, shifts_part = norm_backward(
        normed_slope, unit1, inverse1, vec[1:2, :]
    )
    mixture_low = mixture_slope.astype(BF)
    ml_ref[...] = mixture_low
    for side in range(2):
        back = dot(mixture_low, comb[side], NT).astype(BF)
        for part in range(half // PAIR):
            do_ref[side * (half // PAIR) + part] = back[:, part * PAIR : (part + 1) * PAIR]
    sums = [
        jnp.sum(mixture_slope, axis=0, keepdims=True),
        scales_part,
        shifts_part,
        jnp.sum(summed_slope, axis=0, keepdims=True),
        rescale_part,
        reshift_part,
        jnp.concatenate(threshold_parts, axis=1),
    ]
    return mixture_slope, sums


def attend_backward(meta, turn, flags, q_ref, k_ref, v_ref, ko_ref, vo_ref, marks_ref, closed_ref, ctx_ref, lse_ref, do_ref, sel_ref,
                    dq_ref, dk_ref, dv_ref, dko_ref, dvo_ref, dkl_ref, dvl_ref):
    rows = q_ref.shape[1]
    n_cells = cells_of(meta)
    keys_all = k_ref.shape[1]
    lane = lanes_of(Q_TILE)
    closed_ref[...] = jnp.where(flag_column(meta, flags, turn, rows) > 0.5, HIDE, 0.0)
    dk_ref[...] = jnp.zeros_like(dk_ref)
    dv_ref[...] = jnp.zeros_like(dv_ref)

    def one_tile(tile, start, width):
        at = pl.ds(pl.multiple_of(tile * Q_TILE, Q_TILE), Q_TILE)
        place = own_places(meta, meta[0] * rows + tile * Q_TILE, Q_TILE)
        side = lane % HD
        window = pl.ds(start, width)
        def one_pair(pair, carried):
            q, back = q_ref[pair, at, :], do_ref[pair, at, :]
            qf, backf = q.astype(F32), back.astype(F32)
            k_own, v_own = ko_ref[pair, at, :].astype(F32), vo_ref[pair, at, :].astype(F32)
            k_pair = k_ref[pair, window, :]
            keys = jnp.concatenate([k_pair, marks_ref[window, :]], axis=1)
            vals = jnp.concatenate([v_ref[pair, window, :], jnp.ones((width, PAIR), BF)], axis=1)
            lse = lse_ref[pair, at, :]
            tails = row_tails(place, lse, n_cells)
            delta = head_sums(backf * ctx_ref[pair, at, :].astype(F32))
            high = delta.astype(BF).astype(F32)
            marks = jnp.where(side == 0, -high, jnp.where(side == 1, high - delta, 0.0)).astype(BF)
            q_two, back_two = by_head(q), by_head(back)
            probs = jnp.exp(dot(keys, jnp.concatenate([q_two, tails], axis=1), NT))
            slopes = dot(vals, jnp.concatenate([back_two, by_head(marks)], axis=1), NT)
            score_slope = (probs * slopes).astype(BF)
            dv_ref[pair, window, :] += dot(probs.astype(BF), back_two)
            dk_ref[pair, window, :] += dot(score_slope, q_two)
            dq = merge_heads(dot(score_slope, k_pair, TN))
            self_prob = jnp.exp(head_sums(qf * k_own) + closed_ref[at, :] - lse)
            self_slope = self_prob * (head_sums(backf * v_own) - delta)
            dko_ref[pair, at, :] = self_slope * qf
            dvo_ref[pair, at, :] = self_prob * backf
            dq_ref[pair, at, :] = ((dq + self_slope * k_own) * 0.125).astype(BF)
            return carried

        lax.fori_loop(0, q_ref.shape[0], one_pair, 0, unroll=UNROLL_BACKWARD)

    for_windows(meta, turn, rows, keys_all, one_tile)
    tiles = key_tiles(meta, turn)
    start = pl.multiple_of(meta[0] * rows, rows)
    own = pl.ds(start, rows)
    other = pl.ds(pl.multiple_of(rows - start, rows), rows)
    for count in range(1, keys_all // K_TILE + 1):

        @pl.when(tiles == count)
        def _():
            used = slice(0, count * K_TILE)
            for low_ref, packed_ref, self_ref in ((dkl_ref, dk_ref, dko_ref), (dvl_ref, dv_ref, dvo_ref)):
                packed = jnp.concatenate(
                    [packed_ref[i, used, :].astype(BF) for i in range(packed_ref.shape[0])], axis=1
                )
                low_ref[own, :] = (dot(sel_ref[used, own], packed, TN) + joined(self_ref)).astype(BF)
                low_ref[other, :] = dot(sel_ref[used, other], packed, TN).astype(BF)


def entry_slopes(meta, weights_ref, dq_ref, dkl_ref, dvl_ref, slope_own_ref, slope_oth_ref):
    half = weights_ref.shape[3]
    rows = dq_ref.shape[1]
    start = pl.multiple_of(meta[0] * rows, rows)

    def through(values, part):
        return dot(values[:, :half], weights_ref[0, part], NT) + dot(values[:, half:], weights_ref[1, part], NT)

    def from_keys(at):
        return through(dkl_ref[at, :], 1) + through(dvl_ref[at, :], 2)

    slope_own_ref[...] += through(joined(dq_ref), 0) + from_keys(pl.ds(start, rows))
    slope_oth_ref[...] = from_keys(pl.ds(pl.multiple_of(rows - start, rows), rows)).astype(BF)


class Moves:
    def __init__(self, sems):
        self.sems, self.used = sems, 0

    def start(self, source, target):
        copy = pltpu.make_async_copy(source, target, self.sems.at[self.used])
        self.used += 1
        copy.start()
        return copy


def wait(*copies):
    for copy in copies:
        copy.wait()


def rows_at(index, rows):
    return pl.ds(pl.multiple_of(index * rows, rows), rows)


def gather_entries(moves, meta, i, target):
    rows = i.entry_own.shape[0]
    return [
        moves.start(i.entry_own, target.at[rows_at(meta[0], rows), :]),
        moves.start(i.entry_oth, target.at[rows_at(1 - meta[0], rows), :]),
    ]


def fetch_heads_weights(moves, i, s):
    return [moves.start(i.own, s.weights.at[0]), moves.start(i.oth, s.weights.at[1])]


def fetch_feed_weights(moves, i, s):
    return [
        moves.start(source, target.at[side])
        for target, pair in ((s.comb, (i.comb0, i.comb1)), (s.exp_w, (i.exp0, i.exp1)), (s.red, (i.red0, i.red1)))
        for side, source in enumerate(pair)
    ]


def fetch(moves, i, s, *names):
    return [moves.start(getattr(i, name), getattr(s, name)) for name in names]


def as_row(square):
    return jnp.concatenate([square[r : r + 1, :] for r in range(square.shape[0])], axis=1)


def prepare(i, o, s):
    n_cells = i.lengths.shape[1]
    known = (i.known[...] > 0).astype(F32)
    chosen = (i.chosen[...] > 0).astype(F32)
    seen = jnp.maximum(known, chosen)
    block = known.shape[0]
    both = jnp.concatenate([known, seen], axis=0).astype(BF)
    row = lax.broadcasted_iota(jnp.int32, (PAIR, PAIR), 0)
    lane = lax.broadcasted_iota(jnp.int32, (PAIR, PAIR), 1)
    within = dot(both, (row < lane).astype(BF))
    totals = dot(both, jnp.ones((PAIR, PAIR), BF)).astype(BF)
    row = lax.broadcasted_iota(jnp.int32, (2 * block, 2 * block), 0)
    lane = lax.broadcasted_iota(jnp.int32, (2 * block, 2 * block), 1)
    earlier = ((lane < row) & ((lane < block) == (row < block))).astype(BF)
    places = jnp.where(both.astype(F32) > 0.5, within + dot(earlier, totals), -1.0)
    s.ranks[...] = jnp.concatenate(
        [as_row(places[:block]), as_row(places[block:]), jnp.zeros((6, s.ranks.shape[1]), F32)], axis=0
    )
    s.flags[...] = jnp.concatenate(
        [as_row(known), as_row(seen), as_row(chosen), jnp.zeros((13, s.flags.shape[1]), F32)], axis=0
    ).astype(BF)
    position = lax.broadcasted_iota(jnp.int32, known.shape, 0) * PAIR + lax.broadcasted_iota(jnp.int32, known.shape, 1)
    o.meta[0] = lax.axis_index("tensor").astype(jnp.int32)
    end = 0
    for c in range(n_cells):
        end = end + i.lengths[0, c]
        o.meta[1 + c] = end
        for turn, shown in enumerate((known, seen)):
            count = jnp.sum(jnp.where(position < end, shown, 0.0))
            o.meta[1 + n_cells * (1 + turn) + c] = count.astype(jnp.int32)
    s.vec[...] = jnp.concatenate(
        [
            *(ref[...].reshape(1, -1) for ref in (i.baseline, i.scales, i.shifts, i.adjustment, i.rescales, i.reshifts)),
            jnp.concatenate([i.thr0[...].astype(F32).reshape(1, -1), i.thr1[...].astype(F32).reshape(1, -1)], axis=1),
            jnp.concatenate([i.off0[...], i.off1[...]], axis=1),
            jnp.zeros((7, s.vec.shape[1]), F32),
        ],
        axis=0,
    )


def first_kernel(i, o, s):
    moves, meta = Moves(s.sems), o.meta
    rows = i.entry_own.shape[0]
    weights = fetch_heads_weights(moves, i, s)
    prepare(i, o, s)
    early = gather_entries(moves, meta, i, s.entry_all) + weights
    late = fetch_feed_weights(moves, i, s)
    saved = fetch(moves, s, o, "flags", "ranks", "vec")
    key_marks(meta, 0, s.marks)
    select_keys(meta, 0, s.ranks, s.sel)
    wait(*early)
    entry_own = s.entry_all[rows_at(meta[0], rows), :]
    project(meta, 0, entry_own, s.entry_all, s.weights, s.vec, s.sel, s.q, s.k, s.v, s.ko, s.vo)
    saved += fetch(moves, s, o, "q", "k", "v", "ko", "vo")
    attend(meta, 0, s.flags, s.q, s.k, s.v, s.ko, s.vo, s.marks, s.closed, s.off, s.top, s.edge, s.ctx, s.lse)
    saved += fetch(moves, s, o, "ctx", "lse")
    wait(*late)
    entry_own = s.entry_all[rows_at(meta[0], rows), :]
    result = feed_forward(entry_own, s.ctx, s.comb, s.exp_w, s.red, s.vec, s.before, s.unit1, s.unit2, s.rs)
    low = result.astype(BF)
    chosen = flag_column(meta, s.flags, 2, rows)[:, :1] > 0.5
    s.second[...] = jnp.where(chosen, low, entry_own)
    s.low[...] = low
    saved += fetch(moves, s, o, "second", "low", "before", "unit1", "unit2", "rs")
    wait(*saved)


def second_kernel(i, o, s):
    moves, meta = Moves(s.sems), i.meta
    rows = i.entry_own.shape[0]
    first = fetch(moves, i, s, "ranks", "flags", "vec")
    early = gather_entries(moves, meta, i, s.entry_all) + fetch_heads_weights(moves, i, s)
    late = fetch_feed_weights(moves, i, s) + fetch(moves, i, s, "cotangent")
    key_marks(meta, 1, s.marks)
    wait(*first)
    select_keys(meta, 1, s.ranks, s.sel)
    wait(*early)
    saved = fetch(moves, s, o, "entry_all")
    entry_own = s.entry_all[rows_at(meta[0], rows), :]
    project(meta, 1, entry_own, s.entry_all, s.weights, s.vec, s.sel, s.q, s.k, s.v, s.ko, s.vo)
    attend(meta, 1, s.flags, s.q, s.k, s.v, s.ko, s.vo, s.marks, s.closed, s.off, s.top, s.edge, s.ctx, s.lse)
    saved += fetch(moves, s, o, "ctx")
    wait(*late)
    entry_own = s.entry_all[rows_at(meta[0], rows), :]
    result = feed_forward(entry_own, s.ctx, s.comb, s.exp_w, s.red, s.vec, s.before, s.unit1, s.unit2, s.rs)
    s.low[...] = result.astype(BF)
    saved += fetch(moves, s, o, "low")
    mixture_slope, sums = feed_backward(s.cotangent[...].astype(F32), s.before, s.unit1, s.unit2, s.rs, s.comb, s.exp_w, s.red, s.vec, s.hid, s.sl, s.nl, s.bl, s.ml, s.do)
    s.sums[...] = padded(sums, s.sums)
    s.slope_own[...] = mixture_slope
    saved += fetch(moves, s, o, "hid", "sl", "nl", "bl", "ml", "sums")
    attend_backward(meta, 1, s.flags, s.q, s.k, s.v, s.ko, s.vo, s.marks, s.closed, s.ctx, s.lse, s.do, s.sel,
                    s.dq, s.dk, s.dv, s.dko, s.dvo, s.dkl, s.dvl)
    saved += fetch(moves, s, o, "dq", "dkl", "dvl")
    entry_slopes(meta, s.weights, s.dq, s.dkl, s.dvl, s.slope_own, s.slope_oth)
    saved += fetch(moves, s, o, "slope_oth", "slope_own")
    wait(*saved)


def padded(sums, like):
    return jnp.concatenate(sums + [jnp.zeros((like.shape[0] - len(sums), like.shape[1]), F32)], axis=0)


def side_by_side(matrix, rows):
    return jnp.concatenate([matrix[:rows], matrix[rows:]], axis=1)


def head_weights(meta, entry_all, dq_ref, dk, dv):
    rows = dq_ref.shape[1]
    dq = joined(dq_ref)
    parts = (dot(entry_all[rows_at(meta[0], rows), :], dq, TN), dot(entry_all[...], dk, TN), dot(entry_all[...], dv, TN))
    return parts, jnp.sum(dq.astype(F32), axis=0, keepdims=True), jnp.sum(dv.astype(F32), axis=0, keepdims=True)


def feed_weights(hid_ref, sl_ref, nl_ref, bl_ref, ctx_ref, ml_ref):
    return (
        dot(joined(ctx_ref), ml_ref[...], TN),
        dot(nl_ref[...], bl_ref[...], TN),
        dot(hid_ref[...], sl_ref[...], TN),
    )


def back_kernel(i, o, s):
    moves, meta = Moves(s.sems), i.meta
    first = fetch(moves, i, s, "flags", "cotangent", "slope_recv", "slope_own", "unit2", "rs")
    early = fetch(moves, i, s, "unit1", "vec", "before") + fetch_feed_weights(moves, i, s)
    next_ = fetch(moves, i, s, "ranks", "q", "ctx", "lse", "ko", "vo", "k", "v")
    late = fetch(moves, i, s, "sums2", "ctx2", "ml2", "nl2", "bl2", "hid2", "sl2")
    last = gather_entries(moves, meta, i, s.entry_all) + fetch(moves, i, s, "entry2", "dq2", "dkl2", "dvl2")
    rows = i.slope_own.shape[0]
    half = i.comb0.shape[1] // 2
    key_marks(meta, 0, s.marks)
    wait(*first)
    chosen = flag_column(meta, s.flags, 2, rows)[:, :1] > 0.5
    second_slope = s.slope_own[...] + s.slope_recv[...].astype(F32)
    incoming = s.cotangent[...].astype(F32) + jnp.where(chosen, second_slope, 0.0)
    s.slope[...] = jnp.where(chosen, 0.0, second_slope)
    wait(*early)
    mixture_slope, sums = feed_backward(incoming, s.before, s.unit1, s.unit2, s.rs, s.comb, s.exp_w, s.red, s.vec, s.hid, s.sl, s.nl, s.bl, s.ml, s.do)
    s.slope[...] += mixture_slope
    s.sums[...] = padded(sums, s.sums)
    wait(*next_)
    select_keys(meta, 0, s.ranks, s.sel)
    attend_backward(meta, 0, s.flags, s.q, s.k, s.v, s.ko, s.vo, s.marks, s.closed, s.ctx, s.lse, s.do, s.sel,
                    s.dq, s.dk, s.dv, s.dko, s.dvo, s.dkl, s.dvl)
    saved = fetch(moves, s, o, "slope", "dq", "dkl", "dvl")
    wait(*late)
    for part, (left, right) in enumerate(zip(
        feed_weights(s.hid, s.sl, s.nl, s.bl, s.ctx, s.ml), feed_weights(s.hid2, s.sl2, s.nl2, s.bl2, s.ctx2, s.ml2)
    )):
        total = left + right
        for side, out in ((1, s.feed_oth), (0, s.feed_own)):
            mine = slice(side * half, (side + 1) * half)
            block = side_by_side(total[:, mine], half) if part == 1 else total[mine]
            out[part * half : (part + 1) * half] = block.astype(BF)
    saved += fetch(moves, s, o, "feed_oth", "feed_own")
    wait(*last)
    parts, q_sum, v_sum = head_weights(meta, s.entry_all, s.dq, s.dkl[...], s.dvl[...])
    parts2, q_sum2, v_sum2 = head_weights(meta, s.entry2, s.dq2, s.dkl2[...], s.dvl2[...])
    for c in range(3):
        total = parts[c] + parts2[c]
        for side, out in ((1, s.heads_oth), (0, s.heads_own)):
            cols = slice(side * half, (side + 1) * half)
            out[c * half : (c + 1) * half] = side_by_side(total[:, cols], half).astype(BF)
    s.sums[...] += s.sums2[...]
    s.sums[7:8, :] = q_sum + q_sum2
    s.sums[8:9, :] = v_sum + v_sum2
    saved += fetch(moves, s, o, "heads_oth", "heads_own", "sums")
    wait(*saved)


def slopes_kernel(i, o, s):
    moves = Moves(s.sems)
    wait(*fetch(moves, i, s, "dq", "dkl", "dvl", "slope"), *fetch_heads_weights(moves, i, s))
    entry_slopes(i.meta, s.weights, s.dq, s.dkl, s.dvl, s.slope, s.slope_oth)
    wait(*fetch(moves, s, o, "slope_oth", "slope"))


def call(kernel, micros, ins, outs, scratch):
    spaces = {"s": pltpu.SMEM, "v": pltpu.VMEM, "h": pl.ANY}
    scratch = scratch | {name: like for name, like in outs.items() if name != "meta"}
    in_names, out_names, scratch_names = list(ins), list(outs), list(scratch)

    def body(*refs):
        a, b = len(in_names), len(in_names) + len(out_names)
        kernel(
            types.SimpleNamespace(**dict(zip(in_names, refs[:a]))),
            types.SimpleNamespace(**dict(zip(out_names, refs[a:b]))),
            types.SimpleNamespace(sems=refs[-1], **dict(zip(scratch_names, refs[b:-1]))),
        )

    results = pl.pallas_call(
        body,
        out_shape=[jax.ShapeDtypeStruct(shape, kind) for shape, kind in outs.values()],
        in_specs=[pl.BlockSpec(memory_space=spaces[place]) for _, place in ins.values()],
        out_specs=[pl.BlockSpec(memory_space=pltpu.SMEM if name == "meta" else pl.ANY) for name in outs],
        scratch_shapes=[pltpu.VMEM(shape, kind) for shape, kind in scratch.values()] + [pltpu.SemaphoreType.DMA((48,))],
        compiler_params=pltpu.CompilerParams(vmem_limit_bytes=LIMITS[kernel.__name__] * 2**20),
        cost_estimate=pl.CostEstimate(flops=int(micros * 1.1e9), bytes_accessed=0, transcendentals=0),
    )(*[array for array, _ in ins.values()])
    return dict(zip(out_names, results))


def partner(value):
    return lax.ppermute(value, "tensor", [(0, 1), (1, 0)])


def flip(value, size, step):
    return lax.ppermute(value, "dp", [(i, i ^ step) for i in range(size)])


def tree_sum(parts):
    parts = list(parts)
    while len(parts) > 1:
        parts = [parts[i] + parts[i + 1] for i in range(0, len(parts), 2)]
    return parts[0]


def digits(size):
    out, stride = [], 1
    while stride < size:
        radix = 4 if size % (stride * 4) == 0 else 2
        out.append((stride, radix))
        stride *= radix
    return out


def sum_small(value, size):
    for stride, radix in digits(size):
        parts = [value] + [flip(value, size, k * stride) for k in range(1, radix)]
        value = tree_sum(parts)
    return value


def sum_large(value, size):
    me = lax.axis_index("dp")
    rows, width = value.shape
    order = jnp.arange(size, dtype=jnp.int32) ^ me
    value = jnp.take(value.reshape(size, rows // size, width), order, axis=0)
    shape = [radix for _, radix in digits(size)]
    value = value.reshape(shape[::-1] + [rows // size, width])
    n = len(shape)
    steps = range(n)
    for step in steps:
        stride, radix = digits(size)[step]
        axis = n - 1 - step
        take = lambda k: lax.index_in_dim(value, k, axis, keepdims=True)
        parts = [take(0).astype(F32)] + [flip(take(k), size, k * stride).astype(F32) for k in range(1, radix)]
        value = tree_sum(parts).astype(BF)
    for step in reversed(steps):
        stride, radix = digits(size)[step]
        axis = n - 1 - step
        value = jnp.concatenate([value] + [flip(value, size, k * stride) for k in range(1, radix)], axis=axis)
    value = value.reshape(size, rows // size, width)
    return jnp.take(value, order, axis=0).reshape(rows, width)


QUAD = 4


def target_of(place, first, second):
    return place[0] ^ jnp.where(place[1] == 0, second * QUAD + first, first * QUAD + second)


def spread_kernel(place, ins, out):
    feed_own, feed_recv, heads_own, heads_recv, vec_own, vec_recv = ins
    chunk = feed_own.shape[0] // QUAD**2
    half = vec_own.shape[1] // 2
    own, recv = vec_own[...], vec_recv[...]
    own_side = own[6:9, :half] + recv[6:9, half:]
    vec = jnp.concatenate(
        [own[:6] + recv[:6], jnp.concatenate([own_side, jnp.zeros_like(own_side)], axis=1), jnp.zeros_like(own[9:])], axis=0
    ).astype(BF)
    for first in range(QUAD):
        out[first][2 * QUAD * chunk :, :] = vec
        for second in range(QUAD):
            target = target_of(place, first, second)
            at = pl.ds(pl.multiple_of(target * chunk, 16), chunk)
            for n, (left, right) in enumerate(((feed_own, feed_recv), (heads_own, heads_recv))):
                total = left[at, :].astype(F32) + right[at, :].astype(F32)
                start = (2 * second + n) * chunk
                out[first][start : start + chunk, :] = total.astype(BF)


def added(refs, at):
    parts = [ref[at, :].astype(F32) for ref in refs]
    return (parts[0] + parts[1]) + (parts[2] + parts[3])


def between_kernel(got, out):
    tall = (got[0].shape[0] - 16) // QUAD
    vec = added(got, slice(QUAD * tall, QUAD * tall + 16)).astype(BF)
    for k in range(QUAD):
        out[k][:tall, :] = added(got, slice(k * tall, (k + 1) * tall)).astype(BF)
        out[k][tall:, :] = vec


def ended_kernel(got, out):
    tall = got[0].shape[0] - 16
    out[0][...] = added(got, slice(0, tall)).astype(BF)
    out[1][...] = added(got, slice(tall, tall + 16))


def stack_kernel(got, out):
    for k in range(QUAD):
        out[0][k] = got[k][...]


def unfold(matrix):
    half = matrix.shape[1] // 2
    return jnp.concatenate([matrix[:, :half], matrix[:, half:]], axis=0)


def collect_kernel(place, got, out, s):
    chunk = s.feed.shape[0] // QUAD**2
    rows = s.feed.shape[0] // 3
    for first in range(QUAD):
        for second in range(QUAD):
            target = target_of(place, first, second)
            at = pl.ds(pl.multiple_of(target * chunk, 16), chunk)
            for n, into in enumerate((s.feed, s.heads)):
                into[at, :] = got[first][second, chunk * n : chunk * (n + 1), :].astype(F32)
    for c in range(3):
        out.heads[c] = unfold(s.heads[c * rows : (c + 1) * rows, :])
    out.comb[...] = s.feed[:rows, :]
    out.exp_w[...] = unfold(s.feed[rows : 2 * rows, :])
    out.red[...] = s.feed[2 * rows :, :]


def plain_call(body, args, outs, scratch=()):
    return pl.pallas_call(
        body,
        out_shape=[jax.ShapeDtypeStruct(shape, kind) for shape, kind in outs],
        in_specs=[pl.BlockSpec(memory_space=pltpu.SMEM if a.dtype == jnp.int32 else pltpu.VMEM) for a in args],
        out_specs=[pl.BlockSpec(memory_space=pltpu.VMEM)] * len(outs),
        scratch_shapes=list(scratch),
        compiler_params=pltpu.CompilerParams(vmem_limit_bytes=LIMITS["small"] * 2**20),
    )(*args)


def sum_quads(size, feed, heads, vec, finish, slope):
    rows, width = feed[0].shape
    half = width // 2
    side = lax.axis_index("tensor").astype(jnp.int32)
    place = jnp.stack([lax.axis_index("dp").astype(jnp.int32), side])
    tall = 2 * (rows // QUAD**2)

    def spread_body(*refs):
        spread_kernel(refs[0], refs[1:7], refs[7:])

    def four(kernel):
        return lambda *refs: kernel(refs[:QUAD], refs[QUAD:])

    def exchange(parts, steps):
        got = [parts[0]]
        for k in range(1, QUAD):
            perm = [(2 * n + core, 2 * (n ^ (k * steps[core])) + core) for n in range(size) for core in range(2)]
            got.append(lax.ppermute(parts[k], ("dp", "tensor"), perm))
        return got

    parts = plain_call(spread_body, [place, *feed, *heads, *vec], [((QUAD * tall + 16, width), BF)] * QUAD)
    got = exchange(parts, (1, QUAD))
    got[1], slope = lax.optimization_barrier((got[1], slope))
    beside = finish(slope)
    parts = plain_call(four(between_kernel), got, [((tall + 16, width), BF)] * QUAD)
    total, vectors = plain_call(four(ended_kernel), exchange(parts, (QUAD, 1)), [((tall, width), BF), ((16, width), F32)])
    shared = jnp.where(side == 0, vectors, partner(vectors))
    total, beside = lax.optimization_barrier((total, beside))
    (total,) = plain_call(four(stack_kernel), exchange([total] * QUAD, (QUAD, 1)), [((QUAD, tall, width), BF)])
    got = exchange([total] * QUAD, (1, QUAD))

    def collect_body(*refs):
        outs = types.SimpleNamespace(**dict(zip(("heads", "comb", "exp_w", "red"), refs[5:9])))
        collect_kernel(refs[0], refs[1:5], outs, types.SimpleNamespace(feed=refs[9], heads=refs[10]))

    totals = plain_call(
        collect_body,
        [place, *got],
        [((3, width, half), F32), ((half, width), F32), ((width, half), F32), ((half, width), F32)],
        [pltpu.VMEM((rows, width), F32)] * 2,
    )
    return (*totals, vectors[7:9, :half], vectors[6:7, :half], *(shared[n] for n in range(6))), beside


def sum_any(size, feed, heads, vec, finish, slope):
    half = feed[0].shape[1] // 2
    width = 2 * half
    total = lambda pair: sum_large((pair[0].astype(F32) + pair[1].astype(F32)).astype(BF), size).astype(F32)
    feed, heads = total(feed), total(heads).reshape(3, half, width)
    own, recv = vec
    sides = jnp.pad(own[6:9, :half] + recv[6:9, half:], ((0, 0), (0, half)))
    vec = sum_small(jnp.concatenate([own[:6] + recv[:6], sides], axis=0), size)
    return (
        jnp.stack([unfold(heads[c]) for c in range(3)]), feed[:half], unfold(feed[half : 2 * half]), feed[2 * half :],
        vec[7:9, :half], vec[6:7, :half], *(vec[c : c + 1] for c in range(6)),
    ), finish(slope)


def on_device(dp, tokens, first_cotangent, second_cotangent, projection, offsets, combiner, baseline, scales, shifts,
              expander, thresholds, reducer, adjustment, rescales, reshifts, known_flags, chosen_flags, cell_lengths):
    rows, width = tokens.shape
    group = known_flags.shape[0]
    half = projection.shape[2]
    pairs = 2 * half // PAIR
    n_cells = cell_lengths.shape[1]
    entry_oth, oth, comb1, exp1, red1, offsets_oth, thresholds_oth = (
        partner(v) for v in (tokens, projection, combiner, expander, reducer, offsets, thresholds)
    )
    small_in = {
        "lengths": (cell_lengths, "s"), "known": (known_flags.reshape(-1, PAIR), "v"), "chosen": (chosen_flags.reshape(-1, PAIR), "v"),
        "baseline": (baseline, "v"), "scales": (scales, "v"), "shifts": (shifts, "v"), "adjustment": (adjustment, "v"),
        "rescales": (rescales, "v"), "reshifts": (reshifts, "v"), "thr0": (thresholds, "v"), "thr1": (thresholds_oth, "v"), "off0": (offsets, "v"), "off1": (offsets_oth, "v"),
    }
    square, square32 = ((rows, width), BF), ((rows, width), F32)
    spread = ((rows, PAIR), F32)
    own_pairs, own_pairs32 = ((pairs, rows, PAIR), BF), ((pairs, rows, PAIR), F32)
    all_pairs, all_pairs32 = ((pairs, group, PAIR), BF), ((pairs, group, PAIR), F32)
    entries, grads_like, sums_like = ((group, width), BF), ((3 * half, width), BF), ((16, width), F32)
    square3 = ((3, width, width), F32)
    comb_like, exp_like = ((2,) + combiner.shape, BF), ((2,) + expander.shape, BF)
    weights_like = {"weights": ((2,) + projection.shape, BF), "comb": comb_like, "exp_w": exp_like, "red": comb_like}
    state_like = {
        "entry_all": entries, "sel": ((group, group), BF), "marks": ((group, PAIR), BF), "q": own_pairs, "k": all_pairs, "v": all_pairs,
        "ko": own_pairs, "vo": own_pairs, "ctx": own_pairs, "lse": own_pairs32, "before": square32, "unit1": square32, "unit2": square32, "rs": spread,
    }
    made_like = {"hid": square, "sl": square, "nl": square, "bl": square, "ml": square}
    back_scratch = {"closed": spread, "dk": all_pairs32, "dv": all_pairs32, "dko": own_pairs32, "dvo": own_pairs32}
    slopes_like = {"dq": own_pairs, "dkl": entries, "dvl": entries}
    saved_names = tuple(name for name in state_like if name not in ("entry_all", "sel", "marks"))
    heads_names = ("q", "k", "v", "ko", "vo", "lse", "ctx")
    norm_names = ("before", "unit1", "unit2", "rs")
    closed = {
        "closed": spread, "off": own_pairs32, "top": ((pairs, rows // Q_TILE, 2 * Q_TILE, PAIR), F32), "edge": ((2, 8, PAIR), F32),
    }
    likes = lambda names: {name: state_like[name] for name in names}
    feed_like = {name: weights_like[name] for name in ("comb", "exp_w", "red")}
    small_like = {"flags": ((16, group), BF), "ranks": ((8, group), F32), "vec": sums_like}
    heads_in = {"own": (projection, "h"), "oth": (oth, "h")}
    feed_in = {name: (array, "h") for name, array in (
        ("comb0", combiner), ("comb1", comb1), ("exp0", expander), ("exp1", exp1), ("red0", reducer), ("red1", red1))}
    held = lambda values, *names: {name: (values[name], "h") for name in names}

    one = call(
        first_kernel, 13,
        small_in | {"entry_own": (tokens, "h"), "entry_oth": (entry_oth, "h")} | heads_in | feed_in,
        {"meta": ((1 + 3 * n_cells,), jnp.int32), "low": square, "second": square} | small_like | likes(saved_names),
        closed | weights_like | likes(("entry_all", "sel", "marks")),
    )
    second_oth = partner(one["second"])
    table = {"meta": (one["meta"], "s")} | held(one, *small_like)
    two = call(
        second_kernel, 28,
        table | {"entry_own": (one["second"], "h"), "entry_oth": (second_oth, "h"), "cotangent": (second_cotangent, "h")} | heads_in | feed_in,
        {"low": square, "slope_oth": square, "slope_own": square32, "sums": sums_like} | likes(("entry_all", "ctx")) | made_like | slopes_like,
        closed | small_like | weights_like | state_like | back_scratch | {"cotangent": square, "do": own_pairs},
    )
    slope_recv = partner(two["slope_oth"])
    kept_names = tuple(made_like) + ("ctx", "sums") + tuple(slopes_like)
    kept_like = {name + "2": (made_like | slopes_like | {"ctx": own_pairs, "sums": sums_like})[name] for name in kept_names}
    last = call(
        back_kernel, 25,
        table | feed_in
        | {"entry_own": (tokens, "h"), "entry_oth": (entry_oth, "h"), "cotangent": (first_cotangent, "h"), "slope_recv": (slope_recv, "h")}
        | held(one, *heads_names, *norm_names) | held(two, "slope_own")
        | {name + "2": (two[name], "h") for name in kept_names} | {"entry2": (two["entry_all"], "h")},
        {"slope": square32, "sums": sums_like, "feed_own": grads_like, "feed_oth": grads_like, "heads_own": grads_like, "heads_oth": grads_like}
        | slopes_like,
        small_like | feed_like | made_like | kept_like | state_like | back_scratch
        | {"entry2": entries, "cotangent": square, "slope_recv": square, "slope_own": square32, "do": own_pairs},
    )

    def finish(slope):
        slopes = call(
            slopes_kernel, 4,
            {"meta": (one["meta"], "s"), "slope": (slope, "h")} | heads_in | held(last, *slopes_like),
            {"slope": square32, "slope_oth": square},
            slopes_like | {"weights": weights_like["weights"]},
        )
        return slopes["slope"] + partner(slopes["slope_oth"]).astype(F32)

    summed, tokens_gradient = (sum_quads if dp == QUAD**2 else sum_any)(
        dp,
        (last["feed_own"], partner(last["feed_oth"])),
        (last["heads_own"], partner(last["heads_oth"])),
        (last["sums"], partner(last["sums"])),
        finish,
        last["slope"],
    )
    heads_total, comb_total, exp_total, red_total, off_total, thr_total, *vectors = summed
    base_total, scale_total, shift_total, adjust_total, rescale_total, reshift_total = (v.reshape(-1) for v in vectors)
    return (
        one["low"],
        two["low"],
        tokens_gradient,
        heads_total,
        off_total,
        comb_total,
        base_total,
        scale_total,
        shift_total,
        exp_total,
        thr_total.reshape(-1),
        red_total,
        adjust_total,
        rescale_total,
        reshift_total,
    )


def solution(mesh):
    rows = P(("dp", "tensor"), None)
    return jax.shard_map(
        functools.partial(on_device, mesh.shape["dp"]),
        mesh=mesh,
        in_specs=(
            rows, rows, rows, P(None, None, "tensor"), P(None, "tensor"), P("tensor", None), P(), P(), P(),
            P(None, "tensor"), P("tensor"), P("tensor", None), P(), P(), P(), P("dp"), P("dp"), P("dp", None),
        ),
        out_specs=(
            rows, rows, rows, P(None, None, "tensor"), P(None, "tensor"), P("tensor", None), P(), P(), P(),
            P(None, "tensor"), P("tensor"), P("tensor", None), P(), P(), P(),
        ),
        check_vma=False,
    )
```
